32 devices in a mesh: seq: 16 (over z, y, x), head: 2 (over core).
Axes of the slice: x: 2, y: 2, z: 4, core: 2. Of those that a mesh axis runs over, the one named last changes fastest.
Arguments:
- hidden_in: bfloat16 [2, 4096, 1024], P(None, 'seq', 'head'), may hold values from -6 to 6
- doc_start: int32 [2, 4096], P(None, 'seq'), may hold values from 0 to 1, as said below
- norm_gain: bfloat16 [1024], P('head'), may hold values from 0.5 to 1.5
- proj_gate: bfloat16 [1024, 2048], P(None, 'head'), may hold values from -0.1875 to 0.1875
- proj_value: bfloat16 [1024, 2048], P(None, 'head'), may hold values from -0.1875 to 0.1875
- proj_maps: bfloat16 [1024, 256], P(None, 'head'), may hold values from -0.1875 to 0.1875
- proj_step: bfloat16 [1024, 32], P(None, 'head'), may hold values from -0.1875 to 0.1875
- conv_value: float32 [4, 2048], P(None, 'head'), may hold values from -3 to 3
- value_bias: float32 [2048], P('head'), may hold values from -1.5 to 1.5
- conv_maps: float32 [4, 256], P(None, 'head'), may hold values from -3 to 3
- maps_bias: float32 [256], P('head'), may hold values from -1.5 to 1.5
- step_bias: float32 [32], P('head'), may hold values from -4 to -2
- decay_log: float32 [32], P('head'), may hold values from -12 to 1
- skip_gain: float32 [32], P('head'), may hold values from 0.5 to 1.5
- gate_gain: float32 [2048], P('head'), may hold values from 0.5 to 1.5
- proj_out: bfloat16 [2048, 1024], P('head'), may hold values from -0.125 to 0.125
- out_grad: bfloat16 [2, 4096, 1024], P(None, 'seq', 'head'), may hold values from -6 to 6
Outputs:
- mixed_out: bfloat16 [2, 4096, 1024], P(None, 'seq', 'head')
- input_grad: float32 [2, 4096, 1024], P(None, 'seq', 'head')
- grad_norm_gain: float32 [1024], P('head')
- grad_proj_gate: float32 [1024, 2048], P(None, 'head')
- grad_proj_value: float32 [1024, 2048], P(None, 'head')
- grad_proj_maps: float32 [1024, 256], P(None, 'head')
- grad_proj_step: float32 [1024, 32], P(None, 'head')
- grad_conv_value: float32 [4, 2048], P(None, 'head')
- grad_value_bias: float32 [2048], P('head')
- grad_conv_maps: float32 [4, 256], P(None, 'head')
- grad_maps_bias: float32 [256], P('head')
- grad_step_bias: float32 [32], P('head')
- grad_decay_log: float32 [32], P('head')
- grad_skip_gain: float32 [32], P('head')
- grad_gate_gain: float32 [2048], P('head')
- grad_proj_out: float32 [2048, 1024], P('head')
The draws below stay inside these ranges and needn't reach their ends.
Inputs may be any that keep to these rules, and one draw needn't show every extreme that they name: `doc_start`: position 0 of every sequence is a document start. One sequence, drawn from the seed, holds a single document; the others may have further starts.
All inputs are finite; a program needn't handle non-finite values.
Results may differ from the reference program's by a relative error of at most 0.0065.
The reference program's roundings to bfloat16 on the way count: a program that leaves them out, or rounds other values in their place, can miss the bound.
Values may be sent and summed in bfloat16 or wider, within the bound.
No kernel may reach another device: no remote copies, remote signals or barrier semaphores. Data moves between devices by JAX's collectives and lax.ppermute only.
A program may use at most 256 MiB of HBM per device.

```python
import jax
import jax.numpy as jnp
from jax import lax

D = 1024
N = 128
K = 4
BLOCK = 256
SEQS = 2
DI = 2048
H = 32
LEN = 4096


def clipped_normal(key, shape, scale, limit):
    return jnp.clip(scale * jax.random.normal(key, shape, jnp.float32), -limit, limit)


def draw_hidden_in(key, part):
    key = jax.random.fold_in(key, 21)
    return clipped_normal(key, (SEQS, LEN, D), 1.0, 6.0).astype(jnp.bfloat16)


def draw_out_grad(key, part):
    key = jax.random.fold_in(key, 23)
    return clipped_normal(key, (SEQS, LEN, D), 1.0, 6.0).astype(jnp.bfloat16)


def draw_value_bias(key, part):
    key = jax.random.fold_in(key, 25)
    return clipped_normal(key, (2 * D,), 0.5, 1.5)


def draw_maps_bias(key, part):
    key = jax.random.fold_in(key, 27)
    return clipped_normal(key, (2 * N,), 0.5, 1.5)


def draw_doc_start(key, part):
    key = jax.random.fold_in(key, 11)
    pick_key, start_key = jax.random.split(key)
    whole_seq = jax.random.randint(pick_key, (), 0, SEQS)
    coin_flip = jax.random.randint(start_key, (SEQS, LEN), 0, 4 * BLOCK)
    starts = (coin_flip == 0).astype(jnp.int32)
    position = jnp.arange(LEN)[None, :]
    seq_row = jnp.arange(SEQS)[:, None]
    starts = jnp.where(position == 0, 1, starts)
    starts = jnp.where(seq_row == whole_seq, jnp.where(position == 0, 1, 0), starts)
    return starts.astype(jnp.int32)


def levels(key, shape, shards, smallest, largest):
    def one(dim, parts):
        heights = jax.random.uniform(jax.random.fold_in(jax.random.fold_in(key, 6), dim), (parts,), jnp.float32, smallest / len(shards), largest / len(shards))
        return jnp.repeat(jnp.exp(heights), shape[dim] // parts).reshape((-1,) + (1,) * (len(shape) - dim - 1))

    gain = one(*shards[0])
    for cut in shards[1:]:
        gain = gain * one(*cut)
    return gain


def centred(rng, extent, width, most, cuts=(), held_as=jnp.bfloat16):
    gain = levels(rng, extent, cuts, -0.22, 0.18) if cuts else 1.0
    entries = jax.random.normal(rng, extent, jnp.float32) * width * gain
    return jnp.minimum(jnp.maximum(entries, -most), most).astype(held_as)


def setup_inputs(seed: int = 0) -> dict:
    arg_keys = jax.random.split(jax.random.key(seed), 18)
    return {
        "hidden_in": draw_hidden_in(jax.random.fold_in(arg_keys[17], 71), 0),
        "doc_start": draw_doc_start(jax.random.fold_in(arg_keys[17], 71), 0),
        "norm_gain": jnp.clip(1.0 + 0.1 * jax.random.normal(arg_keys[2], (D,), jnp.float32), 0.5, 1.5).astype(jnp.bfloat16),
        "proj_gate": centred(arg_keys[3], (D, DI), D ** -0.5, 0.1875, ((1, 2),)),
        "proj_value": centred(arg_keys[4], (D, DI), D ** -0.5, 0.1875, ((1, 2),)),
        "proj_maps": centred(arg_keys[5], (D, 2 * N), D ** -0.5, 0.1875, ((1, 2),)),
        "proj_step": centred(arg_keys[6], (D, H), D ** -0.5, 0.1875, ((1, 2),)),
        "conv_value": centred(arg_keys[7], (K, DI), K ** -0.5, 3.0, ((1, 2),), jnp.float32),
        "value_bias": draw_value_bias(jax.random.fold_in(arg_keys[17], 71), 0),
        "conv_maps": centred(arg_keys[9], (K, 2 * N), K ** -0.5, 3.0, ((1, 2),), jnp.float32),
        "maps_bias": draw_maps_bias(jax.random.fold_in(arg_keys[17], 71), 0),
        "step_bias": jnp.clip(-4.0 + 2.0 * jax.random.uniform(arg_keys[11], (H,), jnp.float32) ** levels(arg_keys[11], (H,), ((0, 2),), -0.2, 0.2), -4.0, -2.0),
        "decay_log": jnp.clip(-12.0 + 13.0 * jax.random.uniform(arg_keys[12], (H,), jnp.float32) ** levels(arg_keys[12], (H,), ((0, 2),), -0.2, 0.2), -12.0, 1.0),
        "skip_gain": jnp.clip(0.5 + 1.0 * jax.random.uniform(arg_keys[13], (H,), jnp.float32) ** levels(arg_keys[13], (H,), ((0, 2),), -0.2, 0.2), 0.5, 1.5),
        "gate_gain": jnp.clip(1.0 + 0.1 * jax.random.normal(arg_keys[14], (DI,), jnp.float32), 0.5, 1.5),
        "proj_out": centred(arg_keys[15], (DI, D), DI ** -0.5, 0.125, ((0, 2),)),
        "out_grad": draw_out_grad(jax.random.fold_in(arg_keys[17], 71), 0),
    }


EPS = 1e-05
HIGHEST = lax.Precision.HIGHEST

@jax.custom_vjp
def low(v):
    return lax.optimization_barrier(v.astype(jnp.bfloat16)).astype(jnp.float32)

@jax.custom_vjp
def low_back(v):
    return v

def low_keep(v):
    return (low(v), None)

def low_pass(kept, grad):
    return (grad,)

def back_keep(v):
    return (v, None)

def back_low(kept, grad):
    return (low(grad),)
low.defvjp(low_keep, low_pass)
low_back.defvjp(back_keep, back_low)

def convolve(extended, kernel, kernel_bias, valid_taps):
    block_len = valid_taps.shape[2]
    summed = kernel_bias
    for offset in range(kernel.shape[0]):
        summed = summed + kernel[offset] * extended[:, offset:offset + block_len] * valid_taps[offset][..., None]
    return jax.nn.silu(summed)

def decays(step_pre, decay_log, scores, same_doc, fresh_rows, tail_same):
    step_size = jax.nn.softplus(step_pre)
    decay_rate = -jnp.exp(decay_log)
    cumlog = jnp.transpose(jnp.cumsum(step_size * decay_rate, axis=1), (0, 2, 1))
    step_heads = jnp.transpose(step_size, (0, 2, 1))
    spread = cumlog[..., :, None] - cumlog[..., None, :]
    keep_mask = same_doc[:, None]
    weights = jnp.where(keep_mask, jnp.exp(jnp.where(keep_mask, spread, 0.0)), 0.0) * scores[:, None] * step_heads[:, :, None, :]
    end_weight = jnp.exp(cumlog[..., -1:] - cumlog) * tail_same[:, None] * step_heads
    carry_decay = jnp.exp(cumlog[..., -1]) * fresh_rows[:, -1:]
    entry_decay = jnp.transpose(jnp.exp(cumlog), (0, 2, 1)) * fresh_rows[..., None]
    return (weights, end_weight, carry_decay, entry_decay)

def block_scan(state, inputs, decay_log, skip_gain):
    values_c, write_c, read_c, step_c, starts_c = inputs
    block_len = starts_c.shape[1]
    segment = jnp.cumsum(starts_c, axis=1)
    causal = jnp.arange(block_len)[:, None] >= jnp.arange(block_len)[None, :]
    same_doc = causal[None] & (segment[:, :, None] == segment[:, None, :])
    fresh_rows = (segment == 0).astype(jnp.float32)
    tail_same = (segment == segment[:, -1:]).astype(jnp.float32)
    scores = jnp.einsum('stn,sqn->stq', read_c, write_c, precision=HIGHEST)
    weights, end_weight, carry_decay, entry_decay = decays(step_c, decay_log, scores, same_doc, fresh_rows, tail_same)
    mixing = low(weights)
    diag_out = jnp.einsum('shtq,sqhp->sthp', mixing, values_c, precision=HIGHEST)
    weighted = low(end_weight[..., None] * write_c[:, None])
    local_state = jnp.einsum('sqhp,shqn->shpn', values_c, weighted, precision=HIGHEST)
    carried = jnp.einsum('stn,shpn->sthp', read_c, state, precision=HIGHEST)
    scan_c = diag_out + entry_decay[..., None] * carried + skip_gain[:, None] * values_c
    new_state = carry_decay[..., None, None] * state + local_state
    return (new_state, scan_c)

def forward(residual, doc_start, norm_gain, proj_gate, proj_value, proj_maps, proj_step, conv_value, value_bias, conv_maps, maps_bias, step_bias, decay_log, skip_gain, gate_gain, proj_out):
    seq_count, total_len, model_width = residual.shape
    inner_all = proj_value.shape[1]
    head_count = proj_step.shape[1]
    head_size = inner_all // head_count
    kernel_len = conv_value.shape[0]
    inv_norm = lax.rsqrt(lax.optimization_barrier(jnp.mean(residual * residual, axis=-1, keepdims=True)) + EPS)
    normed = low(residual * inv_norm * norm_gain)
    gate_pre = low_back(jnp.dot(normed, proj_gate, precision=HIGHEST))
    value_pre = low(low_back(jnp.dot(normed, proj_value, precision=HIGHEST)))
    maps_pre = low(low_back(jnp.dot(normed, proj_maps, precision=HIGHEST)))
    step_pre = low_back(jnp.dot(normed, proj_step, precision=HIGHEST)) + step_bias
    mixed = jnp.concatenate([value_pre, maps_pre], axis=-1)
    kernel = jnp.concatenate([conv_value, conv_maps], axis=1)
    kernel_bias = jnp.concatenate([value_bias, maps_bias], axis=0)
    segment = jnp.cumsum(doc_start, axis=1)
    extended = jnp.pad(mixed, ((0, 0), (kernel_len - 1, 0), (0, 0)))
    segment_ext = jnp.concatenate([jnp.full((seq_count, kernel_len - 1), -1, jnp.int32), segment.astype(jnp.int32)], axis=1)
    valid_taps = jnp.stack([segment_ext[:, offset:offset + total_len] == segment for offset in range(kernel_len)], axis=0).astype(jnp.float32)
    activated = convolve(extended, kernel, kernel_bias, valid_taps)
    values = low(activated[..., :inner_all])
    maps_all = low(activated[..., inner_all:])
    state_width = maps_all.shape[-1] // 2
    write_map = maps_all[..., :state_width]
    read_map = maps_all[..., state_width:]
    block_count = total_len // BLOCK

    def split_blocks(source):
        shaped = source.reshape((seq_count, block_count, BLOCK) + source.shape[2:])
        return jnp.moveaxis(shaped, 1, 0)
    inputs = (split_blocks(values.reshape(seq_count, total_len, head_count, head_size)), split_blocks(write_map), split_blocks(read_map), split_blocks(step_pre), split_blocks(doc_start))
    start_state = jnp.zeros((seq_count, head_count, head_size, state_width), jnp.float32)

    def block_step(state, block_inputs):
        return block_scan(state, block_inputs, decay_log, skip_gain)
    final_state, scan_blocks = lax.scan(jax.checkpoint(block_step), start_state, inputs)
    scan_out = low_back(jnp.moveaxis(scan_blocks, 0, 1).reshape(seq_count, total_len, inner_all))
    gate_prod = scan_out * jax.nn.silu(gate_pre)
    inv_gate = lax.rsqrt(lax.optimization_barrier(jnp.mean(gate_prod * gate_prod, axis=-1, keepdims=True)) + EPS)
    normed_out = low(gate_prod * inv_gate * gate_gain)
    return residual + jnp.dot(normed_out, proj_out, precision=HIGHEST)

def reference(hidden_in, doc_start, norm_gain, proj_gate, proj_value, proj_maps, proj_step, conv_value, value_bias, conv_maps, maps_bias, step_bias, decay_log, skip_gain, gate_gain, proj_out, out_grad):
    floats = [source.astype(jnp.float32) for source in (hidden_in, norm_gain, proj_gate, proj_value, proj_maps, proj_step, conv_value, value_bias, conv_maps, maps_bias, step_bias, decay_log, skip_gain, gate_gain, proj_out)]

    def wrapped(residual, gain_in, gate_w, value_w, maps_w, step_w, conv_v, bias_v, conv_m, bias_m, bias_s, log_decay, skip_in, gain_gate, out_w):
        return forward(residual, doc_start, gain_in, gate_w, value_w, maps_w, step_w, conv_v, bias_v, conv_m, bias_m, bias_s, log_decay, skip_in, gain_gate, out_w)
    result, pullback = jax.vjp(wrapped, *floats)
    gradients = pullback(out_grad.astype(jnp.float32))
    return (result.astype(jnp.bfloat16), gradients[0], gradients[1], gradients[2], gradients[3], gradients[4], gradients[5], gradients[6], gradients[7], gradients[8], gradients[9], gradients[10], gradients[11], gradients[12], gradients[13], gradients[14])
```

```python
from functools import partial

import jax
import jax.numpy as jnp
from jax import lax
from jax.sharding import PartitionSpec as P

EPS = 1e-05
HIGHEST = lax.Precision.HIGHEST


def passed_along(shard, axis, by):
    peers = lax.axis_size(axis)
    pairs = [(i, i + by) for i in range(peers) if 0 <= i + by < peers]
    return lax.ppermute(shard, axis, pairs)


def scan_rows(states, decay_rows, reverse):
    count = states.shape[0]
    order = range(count - 1, -1, -1) if reverse else range(count)
    carried = jnp.zeros_like(states[0])
    entering = [None] * count
    for block in order:
        entering[block] = carried
        carried = decay_rows[block][:, None] * carried + states[block]
    return jnp.stack(entering, axis=0)


def exchange_scan(state, decay_rows, axis, reverse):
    count = lax.axis_size(axis)
    width = state.shape[-1]
    rows = state.reshape(count, -1, width)
    spread = lax.all_to_all(rows, axis, 0, 0, tiled=True)
    entering = scan_rows(spread, decay_rows, reverse)
    back = lax.all_to_all(entering, axis, 0, 0, tiled=True)
    return back.reshape(state.shape)


def flip(shard, axis, mask):
    count = lax.axis_size(axis)
    return lax.ppermute(shard, axis, [(i, i ^ mask) for i in range(count)])


def stages(count):
    bits = count.bit_length() - 1
    groups = []
    bit = 0
    while bit < bits:
        take = 2 if bit >= 2 and bit + 2 <= bits else 1
        groups.append((bit, take))
        bit += take
    return groups


def reduce_all(part, axis, order, first_low=True):
    count = lax.axis_size(axis)
    place = lax.axis_index(axis)
    groups = [stages(count)[i] for i in order]
    acc = part
    for turn, (bit, take) in enumerate(groups):
        ways = 1 << take
        piece = acc.shape[0] // ways
        mine = (place >> bit) & (ways - 1)
        kept = lax.dynamic_slice_in_dim(acc, mine * piece, piece, 0)
        for step in range(1, ways):
            sent = lax.dynamic_slice_in_dim(acc, (mine ^ step) * piece, piece, 0)
            if turn == 0 and first_low:
                got = flip(sent.astype(jnp.bfloat16), axis, step << bit).astype(jnp.float32)
            else:
                got = flip(sent, axis, step << bit)
            kept = kept + got
        acc = kept
    acc = acc.astype(jnp.bfloat16)
    for bit, take in reversed(groups):
        ways = 1 << take
        piece = acc.shape[0]
        mine = (place >> bit) & (ways - 1)
        whole = jnp.zeros((piece * ways,) + acc.shape[1:], acc.dtype)
        whole = lax.dynamic_update_slice_in_dim(whole, acc, mine * piece, 0)
        for step in range(1, ways):
            got = flip(acc, axis, step << bit)
            whole = lax.dynamic_update_slice_in_dim(whole, got, (mine ^ step) * piece, 0)
        acc = whole
    return acc.astype(jnp.float32)


def sum_weight(part, axis):
    half = part.shape[0] // 2
    orders = list(range(len(stages(lax.axis_size(axis)))))
    other = [orders[1], orders[0]] + orders[2:]
    return jnp.concatenate(
        [reduce_all(part[:half], axis, orders), reduce_all(part[half:], axis, other)], axis=0
    )


def sum_small(part, axis):
    count = lax.axis_size(axis)
    mask = 1
    while mask < count:
        part = part + flip(part, axis, mask)
        mask *= 2
    return part


def silu_slope(source):
    sigmoid = jax.nn.sigmoid(source)
    return sigmoid * (1.0 + source * (1.0 - sigmoid))


def convolve(extended, kernel, kernel_bias, valid_taps):
    block_len = valid_taps.shape[2]
    summed = kernel_bias
    for offset in range(kernel.shape[0]):
        summed = (
            summed
            + kernel[offset]
            * extended[:, offset : offset + block_len]
            * valid_taps[offset][..., None]
        )
    return jax.nn.silu(summed)


def decays(step_pre, decay_log, scores, same_doc, fresh_rows, tail_same):
    step_size = jax.nn.softplus(step_pre)
    decay_rate = -jnp.exp(decay_log)
    cumlog = jnp.transpose(jnp.cumsum(step_size * decay_rate, axis=1), (0, 2, 1))
    step_heads = jnp.transpose(step_size, (0, 2, 1))
    spread = cumlog[..., :, None] - cumlog[..., None, :]
    keep_mask = same_doc[:, None]
    weights = (
        jnp.where(keep_mask, jnp.exp(jnp.where(keep_mask, spread, 0.0)), 0.0)
        * scores[:, None]
        * step_heads[:, :, None, :]
    )
    end_weight = jnp.exp(cumlog[..., -1:] - cumlog) * tail_same[:, None] * step_heads
    carry_decay = jnp.exp(cumlog[..., -1]) * fresh_rows[:, -1:]
    entry_decay = jnp.transpose(jnp.exp(cumlog), (0, 2, 1)) * fresh_rows[..., None]
    return (weights, end_weight, carry_decay, entry_decay)


def shards(
    hidden_in,
    doc_start,
    norm_gain,
    proj_gate,
    proj_value,
    proj_maps,
    proj_step,
    conv_value,
    value_bias,
    conv_maps,
    maps_bias,
    step_bias,
    decay_log,
    skip_gain,
    gate_gain,
    proj_out,
    out_grad,
):
    hidden_full, gain_full, grad_full = (
        lax.all_gather(hidden_in, "head", axis=2, tiled=True),
        lax.all_gather(norm_gain, "head", axis=0, tiled=True),
        lax.all_gather(out_grad, "head", axis=2, tiled=True),
    )
    seq_count, block_len, model_width = hidden_full.shape
    inner_loc = proj_value.shape[1]
    inner_maps = proj_maps.shape[1]
    head_count = proj_step.shape[1]
    head_size = inner_loc // head_count
    kernel_len = conv_value.shape[0]
    head_devices = lax.axis_size("head")
    inner_all = inner_loc * head_devices
    residual = hidden_full.astype(jnp.float32)
    inv_norm = lax.rsqrt(jnp.mean(residual * residual, axis=-1, keepdims=True) + EPS)
    normed = (residual * inv_norm * gain_full.astype(jnp.float32)).astype(jnp.bfloat16)
    gate_pre = jnp.dot(normed, proj_gate, preferred_element_type=jnp.float32)
    value_pre = jnp.dot(normed, proj_value, preferred_element_type=jnp.float32).astype(jnp.bfloat16)
    maps_pre = jnp.dot(normed, proj_maps, preferred_element_type=jnp.float32).astype(jnp.bfloat16)
    step_pre = jnp.dot(normed, proj_step, preferred_element_type=jnp.float32) + step_bias
    mixed = jnp.concatenate([value_pre, maps_pre], axis=-1)
    kernel = jnp.concatenate([conv_value, conv_maps], axis=1)
    kernel_bias = jnp.concatenate([value_bias, maps_bias], axis=0)
    segment = jnp.cumsum(doc_start, axis=1)
    tail_starts = doc_start[:, block_len - (kernel_len - 1) :]
    after_tail = jnp.cumsum(tail_starts[:, ::-1], axis=1)[:, ::-1] - tail_starts
    tail_keep = (after_tail == 0).astype(jnp.bfloat16)[..., None]
    tail_rows = mixed[:, block_len - (kernel_len - 1) :] * tail_keep
    prior_rows = passed_along(tail_rows, "seq", 1)
    extended = jnp.concatenate([prior_rows, mixed], axis=1).astype(jnp.float32)
    segment_ext = jnp.concatenate(
        [jnp.zeros((seq_count, kernel_len - 1), jnp.int32), segment], axis=1
    )
    valid_taps = jnp.stack(
        [segment_ext[:, offset : offset + block_len] == segment for offset in range(kernel_len)],
        axis=0,
    ).astype(jnp.float32)
    activated, conv_back = jax.vjp(
        partial(convolve, valid_taps=valid_taps), extended, kernel, kernel_bias
    )
    values = activated[..., :inner_loc].astype(jnp.bfloat16)
    maps_local = activated[..., inner_loc:].astype(jnp.bfloat16)
    maps_all = lax.all_gather(maps_local, "head", axis=2, tiled=True)
    state_width = maps_all.shape[2] // 2
    write_map = maps_all[..., :state_width]
    read_map = maps_all[..., state_width:]
    causal = jnp.arange(block_len)[:, None] >= jnp.arange(block_len)[None, :]
    same_doc = causal[None] & (segment[:, :, None] == segment[:, None, :])
    fresh_rows = (segment == 0).astype(jnp.float32)
    tail_same = (segment == segment[:, -1:]).astype(jnp.float32)
    scores = jnp.einsum("stn,sqn->stq", read_map, write_map, preferred_element_type=jnp.float32)
    decay_parts = partial(decays, same_doc=same_doc, fresh_rows=fresh_rows, tail_same=tail_same)
    (weights, end_weight, carry_decay, entry_decay), decay_back = jax.vjp(
        decay_parts, step_pre, decay_log, scores
    )
    mixing = weights.astype(jnp.bfloat16)
    values_h = values.reshape(seq_count, block_len, head_count, head_size)
    diag_out = jnp.einsum("shtq,sqhp->sthp", mixing, values_h, preferred_element_type=jnp.float32)
    write_float = write_map.astype(jnp.float32)
    read_float = read_map.astype(jnp.float32)
    weighted = (end_weight[..., None] * write_float[:, None]).astype(jnp.bfloat16)
    local_state = jnp.einsum(
        "sqhp,shqn->shpn", values_h, weighted, preferred_element_type=jnp.float32
    )
    decay_all = lax.all_gather(carry_decay.reshape(-1), "seq")
    row_count = seq_count * head_count * head_size
    row_decay = jnp.repeat(decay_all, head_size, axis=1)
    share = row_count // lax.axis_size("seq")
    row_decay = lax.dynamic_slice_in_dim(row_decay, lax.axis_index("seq") * share, share, 1)
    incoming = exchange_scan(local_state, row_decay, "seq", False)
    carried = jnp.einsum("stn,shpn->sthp", read_float, incoming, precision=HIGHEST)
    values_float = values_h.astype(jnp.float32)
    scan_out = diag_out + entry_decay[..., None] * carried + skip_gain[:, None] * values_float
    scan_flat = scan_out.reshape(seq_count, block_len, inner_loc)
    gate_act = jax.nn.silu(gate_pre)
    gate_prod = scan_flat * gate_act
    total_sq = lax.psum(jnp.sum(gate_prod * gate_prod, axis=-1), "head")
    inv_gate = lax.rsqrt(total_sq / inner_all + EPS)[..., None]
    gated_norm = gate_prod * inv_gate
    normed_out = (gated_norm * gate_gain).astype(jnp.bfloat16)
    partial_out = jnp.dot(normed_out, proj_out, preferred_element_type=jnp.float32)
    branch = lax.psum_scatter(partial_out, "head", scatter_dimension=2, tiled=True)
    hidden_loc = hidden_in.astype(jnp.float32)
    mixed_out = (hidden_loc + branch).astype(jnp.bfloat16)
    grad_proj_out = jnp.einsum(
        "sqi,sqd->id", normed_out, grad_full, preferred_element_type=jnp.float32
    )
    grad_normed = jnp.einsum("sqd,id->sqi", grad_full, proj_out, preferred_element_type=jnp.float32)
    grad_gate_gain = jnp.sum(grad_normed * gated_norm, axis=(0, 1))
    scaled = grad_normed * gate_gain
    inner_prod = lax.psum(jnp.sum(scaled * gate_prod, axis=-1), "head")
    grad_gated = (
        inv_gate * scaled
        - gate_prod * (inv_gate * inv_gate * inv_gate) * (inner_prod / inner_all)[..., None]
    )
    grad_scan = (
        (grad_gated * gate_act)
        .astype(jnp.bfloat16)
        .reshape(seq_count, block_len, head_count, head_size)
    )
    grad_gate_pre = (grad_gated * scan_flat * silu_slope(gate_pre)).astype(jnp.bfloat16)
    grad_scan_f = grad_scan.astype(jnp.float32)
    grad_skip = jnp.sum(grad_scan_f * values_float, axis=(0, 1, 3))
    grad_mixing = jnp.einsum(
        "sthp,sqhp->shtq", grad_scan, values_h, preferred_element_type=jnp.float32
    )
    grad_values = skip_gain[:, None] * grad_scan_f + jnp.einsum(
        "shtq,sthp->sqhp", mixing, grad_scan, preferred_element_type=jnp.float32
    )
    grad_entry = jnp.sum(grad_scan_f * carried, axis=-1)
    entry_grad = entry_decay[..., None] * grad_scan_f
    state_term = jnp.einsum("sthp,stn->shpn", entry_grad, read_float, precision=HIGHEST)
    grad_read = jnp.einsum("sthp,shpn->stn", entry_grad, incoming, precision=HIGHEST)
    outgoing = exchange_scan(state_term, row_decay, "seq", True)
    grad_carry = jnp.sum(outgoing * incoming, axis=(2, 3))
    grad_values = grad_values + jnp.einsum(
        "shqn,shpn->sqhp", weighted.astype(jnp.float32), outgoing, precision=HIGHEST
    )
    grad_weighted = jnp.einsum("sqhp,shpn->shqn", values_float, outgoing, precision=HIGHEST)
    grad_end = jnp.sum(grad_weighted * write_float[:, None], axis=-1)
    grad_write = jnp.einsum("shqn,shq->sqn", grad_weighted, end_weight)
    grad_step, grad_decay_log, grad_scores = decay_back(
        (grad_mixing, grad_end, grad_carry, grad_entry)
    )
    grad_read = grad_read + jnp.einsum("stq,sqn->stn", grad_scores, write_float, precision=HIGHEST)
    grad_write = grad_write + jnp.einsum("stq,stn->sqn", grad_scores, read_float, precision=HIGHEST)
    grad_maps = lax.psum_scatter(
        jnp.concatenate([grad_write, grad_read], axis=-1), "head", scatter_dimension=2, tiled=True
    )
    grad_activated = jnp.concatenate(
        [grad_values.reshape(seq_count, block_len, inner_loc), grad_maps], axis=-1
    )
    grad_ext, grad_kernel, grad_kernel_bias = conv_back(grad_activated)
    head_rows = grad_ext[:, : kernel_len - 1]
    from_next = passed_along(head_rows, "seq", -1)
    grad_mixed = grad_ext[:, kernel_len - 1 :]
    grad_mixed = grad_mixed.at[:, block_len - (kernel_len - 1) :].add(
        from_next * tail_keep.astype(jnp.float32)
    )
    grad_value_pre = grad_mixed[..., :inner_loc].astype(jnp.bfloat16)
    grad_maps_pre = grad_mixed[..., inner_loc:].astype(jnp.bfloat16)
    grad_step_pre = grad_step.astype(jnp.bfloat16)
    grad_step_bias = jnp.sum(grad_step, axis=(0, 1))
    grad_proj_gate = jnp.einsum(
        "sqd,sqk->dk", normed, grad_gate_pre, preferred_element_type=jnp.float32
    )
    grad_proj_value = jnp.einsum(
        "sqd,sqk->dk", normed, grad_value_pre, preferred_element_type=jnp.float32
    )
    grad_proj_maps = jnp.einsum(
        "sqd,sqk->dk", normed, grad_maps_pre, preferred_element_type=jnp.float32
    )
    grad_proj_step = jnp.einsum(
        "sqd,sqk->dk", normed, grad_step_pre, preferred_element_type=jnp.float32
    )
    grad_in = jnp.einsum(
        "sqk,dk->sqd", grad_gate_pre, proj_gate, preferred_element_type=jnp.float32
    )
    grad_in = grad_in + jnp.einsum(
        "sqk,dk->sqd", grad_value_pre, proj_value, preferred_element_type=jnp.float32
    )
    grad_in = grad_in + jnp.einsum(
        "sqk,dk->sqd", grad_maps_pre, proj_maps, preferred_element_type=jnp.float32
    )
    grad_in = grad_in + jnp.einsum(
        "sqk,dk->sqd", grad_step_pre, proj_step, preferred_element_type=jnp.float32
    )
    row_part = jnp.sum(grad_in * gain_full.astype(jnp.float32) * residual, axis=-1)
    row_tiled = jnp.broadcast_to(row_part[..., None], (seq_count, block_len, head_devices))
    grad_in_loc, row_sum = (
        lax.psum_scatter(grad_in, "head", scatter_dimension=2, tiled=True),
        lax.psum_scatter(row_tiled, "head", scatter_dimension=2, tiled=True),
    )
    grad_norm_gain = jnp.sum(grad_in_loc * hidden_loc * inv_norm, axis=(0, 1))
    grad_normal = grad_in_loc * norm_gain.astype(jnp.float32)
    input_grad = (
        out_grad.astype(jnp.float32)
        + inv_norm * grad_normal
        - hidden_loc * (inv_norm * inv_norm * inv_norm) * (row_sum / model_width)
    )
    grad_conv_value = grad_kernel[:, :inner_loc]
    grad_conv_maps = grad_kernel[:, inner_loc:]
    grad_value_bias = grad_kernel_bias[:inner_loc]
    grad_maps_bias = grad_kernel_bias[inner_loc:]
    grad_proj_gate = sum_weight(grad_proj_gate, "seq")
    grad_proj_value = sum_weight(grad_proj_value, "seq")
    grad_proj_out = sum_weight(grad_proj_out, "seq")
    lanes = 128
    wide = jnp.concatenate([grad_proj_maps, grad_proj_step], axis=1)
    wide = jnp.pad(wide, ((0, 0), (0, -wide.shape[1] % lanes)))
    wide = reduce_all(wide, "seq", list(range(len(stages(lax.axis_size("seq"))))), False)
    grad_proj_maps, grad_proj_step = jnp.split(
        wide[:, : inner_maps + head_count], [inner_maps], axis=1
    )
    smalls = [
        grad_norm_gain,
        grad_conv_value,
        grad_value_bias,
        grad_conv_maps,
        grad_maps_bias,
        grad_step_bias,
        grad_decay_log,
        grad_skip,
        grad_gate_gain,
    ]
    flat = jnp.concatenate([a.reshape(-1) for a in smalls])
    flat = jnp.pad(flat, (0, -flat.shape[0] % (8 * lanes))).reshape(-1, lanes)
    flat = sum_small(flat, "seq").reshape(-1)
    found, start = [], 0
    for a in smalls:
        found.append(flat[start : start + a.size].reshape(a.shape))
        start += a.size
    (
        grad_norm_gain,
        grad_conv_value,
        grad_value_bias,
        grad_conv_maps,
        grad_maps_bias,
        grad_step_bias,
        grad_decay_log,
        grad_skip,
        grad_gate_gain,
    ) = found
    return (
        mixed_out,
        input_grad,
        grad_norm_gain,
        grad_proj_gate,
        grad_proj_value,
        grad_proj_maps,
        grad_proj_step,
        grad_conv_value,
        grad_value_bias,
        grad_conv_maps,
        grad_maps_bias,
        grad_step_bias,
        grad_decay_log,
        grad_skip,
        grad_gate_gain,
        grad_proj_out,
    )


def solution(mesh):
    placed = (
        P(None, "seq", "head"),
        P(None, "seq"),
        P("head"),
        P(None, "head"),
        P(None, "head"),
        P(None, "head"),
        P(None, "head"),
        P(None, "head"),
        P("head"),
        P(None, "head"),
        P("head"),
        P("head"),
        P("head"),
        P("head"),
        P("head"),
        P("head", None),
        P(None, "seq", "head"),
    )
    return jax.shard_map(
        shards,
        mesh=mesh,
        in_specs=placed,
        out_specs=(
            P(None, "seq", "head"),
            P(None, "seq", "head"),
            P("head"),
            P(None, "head"),
            P(None, "head"),
            P(None, "head"),
            P(None, "head"),
            P(None, "head"),
            P("head"),
            P(None, "head"),
            P("head"),
            P("head"),
            P("head"),
            P("head"),
            P("head"),
            P("head", None),
        ),
        check_vma=False,
    )
```

```python
from functools import partial

import jax
import jax.numpy as jnp
from jax import lax
from jax.experimental import pallas as pl
from jax.experimental.pallas import tpu as pltpu
from jax.sharding import PartitionSpec as P

EPS = 1e-05
HIGHEST = lax.Precision.HIGHEST
F32 = jnp.float32
BF16 = jnp.bfloat16
LANES = 128
PAD = 16
NEVER = -1e30
SENT_IN, BACK_IN, SENT_OUT, BACK_OUT = F32, F32, F32, F32


def passed_along(shard, axis, by):
    peers = lax.axis_size(axis)
    pairs = [(i, i + by) for i in range(peers) if 0 <= i + by < peers]
    return lax.ppermute(shard, axis, pairs)


def flip(shard, axis, mask):
    count = lax.axis_size(axis)
    return lax.ppermute(shard, axis, [(i, i ^ mask) for i in range(count)])


def dot(a, b, ca=1, cb=0):
    return lax.dot_general(a, b, (((ca,), (cb,)), ((), ())), preferred_element_type=F32)


def halves(a):
    high = a.astype(BF16)
    return high, (a - high.astype(F32)).astype(BF16)


def dot_wide(a, b, ca=1, cb=0):
    high, low = halves(a)
    return dot(high, b, ca, cb) + dot(low, b, ca, cb)


def dot_right(a, b, ca=1, cb=0):
    if b.dtype == BF16:
        return dot(a, b, ca, cb)
    high, low = halves(b)
    return dot(a, high, ca, cb) + dot(a, low, ca, cb)


def dot_both(a, b, ca=1, cb=0):
    if b.dtype == BF16:
        return dot_wide(a, b, ca, cb)
    high, low = halves(b)
    return dot_wide(a, high, ca, cb) + dot(a.astype(BF16), low, ca, cb)


def silu_slope(source):
    sigmoid = jax.nn.sigmoid(source)
    return sigmoid * (1.0 + source * (1.0 - sigmoid))


def shifted(pre_ref, prior_ref):
    ext = jnp.concatenate([prior_ref[0].astype(F32), pre_ref[0].astype(F32)], axis=0)
    block_len = pre_ref.shape[1]
    return [ext[PAD - 3 + i : PAD - 3 + i + block_len] for i in range(4)]


def convolved(taps, kernel_ref, bias_ref, valid):
    summed = bias_ref[...]
    for i in range(4):
        summed = summed + kernel_ref[i : i + 1, :] * taps[i] * valid[:, i : i + 1]
    return summed


def local_kernel(head_size, pre_ref, prior_ref, kernel_ref, bias_ref, valid_ref, write_ref, col_ref, decay_ref, values_ref, state_ref):
    taps = shifted(pre_ref, prior_ref)
    summed = convolved(taps, kernel_ref, bias_ref, valid_ref[0])
    values = (summed * jax.nn.sigmoid(summed)).astype(BF16)
    values_ref[0] = values
    write = write_ref[0].astype(F32)
    parts = []
    for a in range(2):
        weighted = (col_ref[0, 0, :, 2 + a : 3 + a] * write).astype(BF16)
        parts.append(dot(weighted, values[:, a * head_size : (a + 1) * head_size], 0, 0))
    width = write.shape[1]
    state_ref[0, :width] = jnp.concatenate(parts, axis=1).astype(state_ref.dtype)
    state_ref[0, width:] = decay_ref[0]


def kept_mask(seg_col, seg_row):
    block_len = seg_col.shape[0]
    later = lax.broadcasted_iota(jnp.int32, (block_len, block_len), 0)
    earlier = lax.broadcasted_iota(jnp.int32, (block_len, block_len), 1)
    return (later >= earlier) & (seg_col == seg_row)


def diag_kernel(head_size, values_ref, write_ref, read_ref, col_ref, row_ref, skip_ref, out_ref, scores_ref):
    @pl.when(pl.program_id(1) == 0)
    def _():
        scores_ref[...] = dot(read_ref[0], write_ref[0], 1, 1)

    keep = kept_mask(col_ref[0, 0, :, 6:7], row_ref[0, 0, 4:5, :])
    values = values_ref[0]
    parts = []
    for a in range(2):
        spread = col_ref[0, 0, :, a : a + 1] - row_ref[0, 0, a : a + 1, :]
        decay = jnp.exp(jnp.where(keep, spread, NEVER))
        mixing = (decay * scores_ref[...] * row_ref[0, 0, 2 + a : 3 + a, :]).astype(BF16)
        parts.append(dot(mixing, values[:, a * head_size : (a + 1) * head_size]))
    out_ref[0] = jnp.concatenate(parts, axis=1) + skip_ref[...] * values.astype(F32)


def by_head(col_ref, first, head_size):
    lane = lax.broadcasted_iota(jnp.int32, (1, 2 * head_size), 1)
    return jnp.where(
        lane < head_size, col_ref[0, 0, :, first : first + 1], col_ref[0, 0, :, first + 1 : first + 2]
    )


def gate_kernel(head_size, diag_ref, read_ref, inc_ref, col_ref, gate_ref, back_ref, gain_ref, scan_ref, sums_ref):
    carried = dot_right(read_ref[0], inc_ref[0])
    scan = diag_ref[0] + by_head(col_ref, 4, head_size) * carried
    scan_ref[0] = scan
    gate = gate_ref[0]
    prod = scan * (gate * jax.nn.sigmoid(gate))
    square = jnp.sum(prod * prod, axis=1, keepdims=True)
    inner = jnp.sum(back_ref[0] * gain_ref[...] * prod, axis=1, keepdims=True)
    both = jnp.concatenate([square, inner], axis=1)

    @pl.when(pl.program_id(1) == 0)
    def _():
        sums_ref[0] = both

    @pl.when(pl.program_id(1) > 0)
    def _():
        sums_ref[0] += both


def back_kernel(head_size, inner_all, scan_ref, gate_ref, back_ref, gain_ref, sums_ref, values_ref, read_ref, col_ref, normed_ref, gscan_ref, ggate_ref, state_ref, rows_ref):
    inv = lax.rsqrt(sums_ref[0, :, 0:1] / inner_all + EPS)
    inner = sums_ref[0, :, 1:2] / inner_all
    scan, gate, back = scan_ref[0], gate_ref[0], back_ref[0]
    gain = gain_ref[...]
    sigmoid = jax.nn.sigmoid(gate)
    act = gate * sigmoid
    prod = scan * act
    gated_norm = prod * inv
    normed_ref[0] = (gated_norm * gain).astype(BF16)
    grad = inv * (back * gain) - prod * (inv * inv * inv) * inner
    gscan = (grad * act).astype(BF16)
    gscan_ref[0] = gscan
    ggate_ref[0] = (grad * scan * (sigmoid * (1.0 + gate * (1.0 - sigmoid)))).astype(BF16)
    gscan = gscan.astype(F32)
    gain_row = jnp.sum(back * gated_norm, axis=0, keepdims=True)
    skip_row = jnp.sum(gscan * values_ref[0].astype(F32), axis=0, keepdims=True)
    rows_ref[0] = jnp.concatenate([gain_row, skip_row], axis=0)
    entry = by_head(col_ref, 4, head_size) * gscan
    high, low = halves(entry)
    state_ref[0] = (dot(read_ref[0], high, 0, 0) + dot(read_ref[0], low, 0, 0)).astype(state_ref.dtype)


def mix_back_kernel(head_size, gscan_ref, values_ref, write_ref, read_ref, inc_ref, col_ref, row_ref, skip_ref, gvalues_ref, gread_ref, gwrite_ref, dcol_ref, drow_ref, scores_ref, gscores_ref):
    turn = pl.program_id(1)

    @pl.when(turn == 0)
    def _():
        scores_ref[...] = dot(read_ref[0], write_ref[0], 1, 1)
        gscores_ref[...] = jnp.zeros_like(gscores_ref)
        gread_ref[...] = jnp.zeros_like(gread_ref)

    keep = kept_mask(col_ref[0, 0, :, 6:7], row_ref[0, 0, 4:5, :])
    values, gscan = values_ref[0], gscan_ref[0]
    gscan_f = gscan.astype(F32)
    scores = scores_ref[...]
    parts, cols, rows = [], [], []
    for a in range(2):
        part = slice(a * head_size, (a + 1) * head_size)
        step = row_ref[0, 0, 2 + a : 3 + a, :]
        spread = col_ref[0, 0, :, a : a + 1] - row_ref[0, 0, a : a + 1, :]
        decay = jnp.exp(jnp.where(keep, spread, NEVER))
        mixing = (decay * scores * step).astype(BF16)
        parts.append(dot(mixing, gscan[:, part], 0, 0))
        grad = dot(gscan[:, part], values[:, part], 1, 1)
        pulled = grad * decay
        plain = pulled * scores
        stepped = pulled * step
        gscores_ref[...] += stepped
        cols.append(jnp.sum(stepped * scores, axis=1, keepdims=True))
        rows.append(jnp.sum(plain, axis=0, keepdims=True))
    gvalues_ref[0] = skip_ref[...] * gscan_f + jnp.concatenate(parts, axis=1)
    carried = dot_right(read_ref[0], inc_ref[0])
    entered = gscan_f * carried
    entry = by_head(col_ref, 4, head_size) * gscan_f
    gread_ref[0] += dot_both(entry, inc_ref[0], 1, 1)
    for a in range(2):
        cols.append(jnp.sum(entered[:, a * head_size : (a + 1) * head_size], axis=1, keepdims=True))
    dcol_ref[0, 0] = jnp.concatenate(cols, axis=1)
    drow_ref[0, 0] = jnp.concatenate(rows, axis=0)

    @pl.when(turn == pl.num_programs(1) - 1)
    def _():
        gread_ref[0] += dot_wide(gscores_ref[...], write_ref[0])
        gwrite_ref[0] = dot_wide(gscores_ref[...], read_ref[0], 0, 0)


def state_back_kernel(head_size, out_ref, inc_ref, values_ref, write_ref, col_ref, gpart_ref, gwpart_ref, pre_ref, prior_ref, kernel_ref, bias_ref, valid_ref, gpre_ref, tail_ref, head_ref, rows_ref, gwrite_ref, gend_ref):
    turn = pl.program_id(1)
    outgoing = out_ref[0]
    values = values_ref[0]
    write = write_ref[0].astype(F32)
    parts, ends, total = [], [], None
    for a in range(2):
        part = slice(a * head_size, (a + 1) * head_size)
        end = col_ref[0, 0, :, 2 + a : 3 + a]
        weighted = (end * write).astype(BF16)
        parts.append(dot_right(weighted, outgoing[:, part]))
        gweighted = dot_right(values[:, part], outgoing[:, part], 1, 1)
        ends.append(jnp.sum(gweighted * write, axis=1, keepdims=True))
        total = gweighted * end if total is None else total + gweighted * end
    gend_ref[0, 0] = jnp.concatenate(ends, axis=1)

    @pl.when(turn == 0)
    def _():
        gwrite_ref[0] = gwpart_ref[0] + total

    @pl.when(turn > 0)
    def _():
        gwrite_ref[0] += total

    gvalues = gpart_ref[0] + jnp.concatenate(parts, axis=1)
    taps = shifted(pre_ref, prior_ref)
    valid = valid_ref[0]
    source = convolved(taps, kernel_ref, bias_ref, valid)
    grad = gvalues * silu_slope(source)
    block_len = grad.shape[0]
    blank = jnp.zeros((PAD, grad.shape[1]), F32)
    rows, summed = [], None
    for i in range(4):
        held = grad * valid[:, i : i + 1]
        rows.append(jnp.sum(held * taps[i], axis=0, keepdims=True))
        padded = jnp.concatenate([blank, kernel_ref[i : i + 1, :] * held, blank], axis=0)
        moved = padded[3 - i : 3 - i + block_len + PAD]
        summed = moved if summed is None else summed + moved
    rows.append(jnp.sum(grad, axis=0, keepdims=True))
    rows.append(jnp.sum(outgoing.astype(F32) * inc_ref[0].astype(F32), axis=0, keepdims=True))
    rows_ref[0] = jnp.concatenate(rows, axis=0)
    head_ref[0] = summed[:PAD]
    own = summed[PAD:]
    gpre_ref[0] = own.astype(BF16)
    tail_ref[0] = own[block_len - PAD :]


def scan_kernel(reverse, width, states_ref, decay_ref, out_ref):
    count = states_ref.shape[0]

    def one(turn, carried):
        block = count - 1 - turn if reverse else turn
        out_ref[pl.ds(block, 1)] = carried[None].astype(out_ref.dtype)
        parts = decay_ref[pl.ds(block, 1)][0, width:].astype(F32)
        decay = parts[0:1] + parts[1:2] + parts[2:3]
        return decay * carried + states_ref[pl.ds(block, 1)][0, :width].astype(F32)

    lax.fori_loop(0, count, one, jnp.zeros(out_ref.shape[1:], F32))


def vmem(mib):
    return pltpu.CompilerParams(vmem_limit_bytes=mib << 20)


def scanned(states, decays, width, reverse, kind):
    count, _, share = states.shape
    return pl.pallas_call(
        partial(scan_kernel, reverse, width),
        out_shape=jax.ShapeDtypeStruct((count, width, share), kind),
        compiler_params=vmem(32),
    )(states, decays)


def to_shares(rows, count):
    pairs, width, lanes = rows.shape
    if pairs == count:
        return rows
    cut = count // pairs
    split = rows.reshape(pairs, width, cut, lanes // cut)
    return jnp.transpose(split, (0, 2, 1, 3)).reshape(count, width, lanes // cut)


def from_shares(shares, pairs):
    count, width, share = shares.shape
    if pairs == count:
        return shares
    cut = count // pairs
    split = shares.reshape(pairs, cut, width, share)
    return jnp.transpose(split, (0, 2, 1, 3)).reshape(pairs, width, cut * share)


def swap(shares, axis):
    return lax.all_to_all(shares, axis, 0, 0, tiled=True)


def ordered(own, got, bit):
    return jnp.where(
        bit == 0, jnp.concatenate([own, got], axis=0), jnp.concatenate([got, own], axis=0)
    )


class Summing:
    def __init__(self, axis):
        self.axis = axis
        count = lax.axis_size(axis)
        self.place = lax.axis_index(axis)
        self.rest = [1 << b for b in range(2, count.bit_length() - 1)]

    def bit(self, mask):
        return (self.place & mask) // mask

    def halved(self, acc, mask):
        piece = acc.shape[0] // 2
        bit = self.bit(mask)
        sent = lax.dynamic_slice_in_dim(acc, (1 - bit) * piece, piece, 0)
        kept = lax.dynamic_slice_in_dim(acc, bit * piece, piece, 0)
        return kept + flip(sent, self.axis, mask)

    def send(self, product_a, product_b):
        got_a = flip(product_a(1 - self.bit(1)).astype(BF16), self.axis, 1)
        got_b = flip(product_b(1 - self.bit(2)).astype(BF16), self.axis, 2)
        return got_a, got_b

    def keep(self, product_a, product_b, got):
        return (
            product_a(self.bit(1)) + got[0].astype(F32),
            product_b(self.bit(2)) + got[1].astype(F32),
        )

    def across(self, acc_a, acc_b):
        return jnp.concatenate([self.halved(acc_a, 2), self.halved(acc_b, 1)], axis=0)


    def grown(self, own, mask):
        return ordered(own, flip(own, self.axis, mask), self.bit(mask))

    def split(self, acc):
        half = acc.shape[0] // 2
        return self.grown(acc[:half], 2), self.grown(acc[half:], 1)

    def whole(self, part_a, part_b):
        return self.grown(part_a, 1), self.grown(part_b, 2)


def sum_small(part, axis):
    count = lax.axis_size(axis)
    mask = 1
    while mask < count:
        part = part + flip(part, axis, mask)
        mask *= 2
    return part


def together(core, own):
    other = lax.ppermute(own, "head", [(0, 1), (1, 0)])
    return jnp.where(
        core == 0,
        jnp.concatenate([own, other], axis=-1),
        jnp.concatenate([other, own], axis=-1),
    )


def after(array, *others):
    return lax.optimization_barrier((array, *others))[0]


def columns(array, start, size):
    return lax.dynamic_slice_in_dim(array, start, size, 1)


def shards(
    hidden_in,
    doc_start,
    norm_gain,
    proj_gate,
    proj_value,
    proj_maps,
    proj_step,
    conv_value,
    value_bias,
    conv_maps,
    maps_bias,
    step_bias,
    decay_log,
    skip_gain,
    gate_gain,
    proj_out,
    out_grad,
):
    core = lax.axis_index("head")
    count = lax.axis_size("seq")
    seqs, block_len, half_width = hidden_in.shape
    inner = proj_value.shape[1]
    heads = proj_step.shape[1]
    head_size = inner // heads
    kernel_len = conv_value.shape[0]
    head_devices = lax.axis_size("head")
    inner_all = inner * head_devices
    model_width = half_width * head_devices
    width = proj_maps.shape[1] * head_devices // 2
    pairs = inner // LANES
    tokens = seqs * block_len

    hidden_full = together(core, hidden_in)
    gain_full = lax.all_gather(norm_gain, "head", axis=0, tiled=True).astype(F32)

    tril = jnp.tril(jnp.ones((block_len, block_len), F32))
    segment = jnp.round(jnp.einsum("tq,sq->st", tril, doc_start.astype(F32), precision=HIGHEST))
    tail_starts = doc_start[:, block_len - (kernel_len - 1) :]
    after_tail = jnp.cumsum(tail_starts[:, ::-1], axis=1)[:, ::-1] - tail_starts
    tail_keep = (after_tail == 0).astype(F32)[..., None]
    tail_rows = hidden_full[:, block_len - (kernel_len - 1) :] * tail_keep.astype(BF16)
    prior_hidden = passed_along(tail_rows, "seq", 1)
    prior_hidden = jnp.pad(prior_hidden, ((0, 0), (PAD - (kernel_len - 1), 0), (0, 0)))
    segment_ext = jnp.concatenate([jnp.zeros((seqs, kernel_len - 1), F32), segment], axis=1)
    valid = jnp.stack(
        [segment_ext[:, i : i + block_len] == segment for i in range(kernel_len)], axis=-1
    ).astype(F32)

    def normalize(rows):
        residual = rows.astype(F32)
        inv = lax.rsqrt(jnp.mean(residual * residual, axis=-1, keepdims=True) + EPS)
        return residual, inv, (residual * inv * gain_full).astype(BF16)

    residual, inv_norm, normed = normalize(hidden_full)
    normed_prior = normalize(prior_hidden)[2]

    def project(rows, weight):
        return jnp.dot(rows, weight, preferred_element_type=F32)

    maps_pre = project(normed, proj_maps).astype(BF16)
    maps_prior = project(normed_prior, proj_maps).astype(BF16)
    step_pre = project(normed, proj_step) + step_bias
    value_pre = project(normed, proj_value).astype(BF16)
    value_prior = project(normed_prior, proj_value).astype(BF16)

    def convolve(extended, kernel, bias):
        summed = bias
        for i in range(kernel_len):
            summed = summed + kernel[i] * extended[:, i : i + block_len] * valid[..., i : i + 1]
        return jax.nn.silu(summed)

    maps_ext = jnp.concatenate(
        [maps_prior[:, PAD - (kernel_len - 1) :], maps_pre], axis=1
    ).astype(F32)
    maps_act, maps_back = jax.vjp(convolve, maps_ext, conv_maps, maps_bias)
    maps_all = lax.all_gather(maps_act.astype(BF16), "head", axis=2, tiled=True)
    write_map, read_map = maps_all[..., :width], maps_all[..., width:]

    step_size = jax.nn.softplus(step_pre)
    decay_rate = -jnp.exp(decay_log)
    cumlog = jnp.einsum("tq,sqh->sth", tril, step_size * decay_rate, precision=HIGHEST)
    fresh = (segment == 0).astype(F32)[..., None]
    tail_same = (segment == segment[:, -1:]).astype(F32)[..., None]
    end_plain = jnp.exp(cumlog[:, -1:] - cumlog) * tail_same
    end_weight = end_plain * step_size
    carry_decay = jnp.exp(cumlog[:, -1]) * fresh[:, -1]
    entry_decay = jnp.exp(cumlog) * fresh

    def paired(a):
        return jnp.transpose(a.reshape(seqs, block_len, pairs, heads // pairs), (0, 2, 1, 3))

    seg_pairs = jnp.broadcast_to(segment[:, None, :, None], (seqs, pairs, block_len, 2))
    col_pack = jnp.concatenate(
        [paired(cumlog), paired(end_weight), paired(entry_decay), seg_pairs], axis=-1
    )
    row_pack = jnp.swapaxes(
        jnp.concatenate([paired(cumlog), paired(step_size), seg_pairs, seg_pairs], axis=-1), 2, 3
    )
    carry_lanes = jnp.repeat(carry_decay.reshape(seqs * pairs, 1, -1), head_size, axis=2)
    first = carry_lanes.astype(BF16).astype(F32)
    second = (carry_lanes - first).astype(BF16).astype(F32)
    third = carry_lanes - first - second
    decay_rows = jnp.concatenate(
        [first, second, third, jnp.zeros((seqs * pairs, PAD - 3, LANES), F32)], axis=1
    ).astype(SENT_IN)
    skip_row = jnp.repeat(skip_gain, head_size)[None]
    bias_row = value_bias[None]
    gain_row = gate_gain[None]

    grid = (seqs, pairs)
    wide = pl.BlockSpec((1, block_len, LANES), lambda s, j: (s, 0, j))
    prior = pl.BlockSpec((1, PAD, LANES), lambda s, j: (s, 0, j))
    shared = pl.BlockSpec((1, block_len, width), lambda s, j: (s, 0, 0))
    taps4 = pl.BlockSpec((kernel_len, LANES), lambda s, j: (0, j))
    lane_row = pl.BlockSpec((1, LANES), lambda s, j: (0, j))
    valids = pl.BlockSpec((1, block_len, kernel_len), lambda s, j: (s, 0, 0))
    cols8 = pl.BlockSpec((1, 1, block_len, 8), lambda s, j: (s, j, 0, 0))
    rows8 = pl.BlockSpec((1, 1, 8, block_len), lambda s, j: (s, j, 0, 0))
    pair = pl.BlockSpec((1, width, LANES), lambda s, j: (s * pairs + j, 0, 0))
    pair_ext = pl.BlockSpec((1, width + PAD, LANES), lambda s, j: (s * pairs + j, 0, 0))
    pair_tail = pl.BlockSpec((1, PAD, LANES), lambda s, j: (s * pairs + j, 0, 0))
    two = pl.BlockSpec((1, block_len, 2), lambda s, j: (s, 0, 0))

    def shape(*dims, dtype=F32):
        return jax.ShapeDtypeStruct(dims, dtype)

    like_values = shape(seqs, block_len, inner, dtype=BF16)
    like_float = shape(seqs, block_len, inner)
    like_states = shape(seqs * pairs, width, LANES, dtype=SENT_OUT)
    like_map = shape(seqs, block_len, width)

    values, payload = pl.pallas_call(
        partial(local_kernel, head_size),
        grid=grid,
        in_specs=[wide, prior, taps4, lane_row, valids, shared, cols8, pair_tail],
        out_specs=[wide, pair_ext],
        out_shape=[like_values, shape(seqs * pairs, width + PAD, LANES, dtype=SENT_IN)],
        compiler_params=vmem(32),
    )(value_pre, value_prior, conv_value, bias_row, valid, write_map, col_pack, decay_rows)

    spread_in = swap(to_shares(payload, count), "seq")

    gate_pre = project(normed, proj_gate)
    grad_full = together(core, out_grad)
    grad_normed = jnp.einsum("sqd,id->sqi", grad_full, proj_out, preferred_element_type=F32)
    diag = pl.pallas_call(
        partial(diag_kernel, head_size),
        grid=grid,
        in_specs=[wide, shared, shared, cols8, rows8, lane_row],
        out_specs=wide,
        out_shape=like_float,
        scratch_shapes=[pltpu.VMEM((block_len, block_len), F32)],
        compiler_params=vmem(32),
    )(values, write_map, read_map, col_pack, row_pack, skip_row)

    spread_in = after(spread_in, gate_pre, grad_normed, row_pack)
    incoming = from_shares(swap(scanned(spread_in, spread_in, width, False, BACK_IN), "seq"), seqs * pairs)

    scan_out, sums = pl.pallas_call(
        partial(gate_kernel, head_size),
        grid=grid,
        in_specs=[wide, shared, pair, cols8, wide, wide, lane_row],
        out_specs=[wide, two],
        out_shape=[like_float, shape(seqs, block_len, 2)],
        compiler_params=vmem(32),
    )(diag, read_map, incoming, col_pack, gate_pre, grad_normed, gain_row)
    sums = lax.psum(sums, "head")

    rows2 = pl.BlockSpec((1, 2, LANES), lambda s, j: (s, 0, j))
    normed_out, grad_scan, grad_gate_pre, state_term, gate_rows = pl.pallas_call(
        partial(back_kernel, head_size, inner_all),
        grid=grid,
        in_specs=[wide, wide, wide, lane_row, two, wide, shared, cols8],
        out_specs=[wide, wide, wide, pair, rows2],
        out_shape=[like_values, like_values, like_values, like_states, shape(seqs, 2, inner)],
        compiler_params=vmem(32),
    )(scan_out, gate_pre, grad_normed, gain_row, sums, values, read_map, col_pack)

    spread_out = swap(to_shares(state_term, count), "seq")

    flat = lambda a: a.reshape(tokens, a.shape[-1])
    normed_flat, out_flat = flat(normed), flat(normed_out)
    grad_flat, ggate_flat = flat(grad_full), flat(grad_gate_pre)

    def product(left, right):
        half = left.shape[1] // 2

        def one(bit):
            return dot(columns(left, bit * half, half), right, 0, 0)

        return one

    summing = Summing("seq")
    early = product(out_flat, grad_flat), product(normed_flat, ggate_flat)
    early_got = summing.send(*early)

    grad_values, grad_read, grad_write, dcol, drow = pl.pallas_call(
        partial(mix_back_kernel, head_size),
        grid=grid,
        in_specs=[wide, wide, shared, shared, pair, cols8, rows8, lane_row],
        out_specs=[
            wide,
            shared,
            shared,
            pl.BlockSpec((1, 1, block_len, 4), lambda s, j: (s, j, 0, 0)),
            pl.BlockSpec((1, 1, 2, block_len), lambda s, j: (s, j, 0, 0)),
        ],
        out_shape=[
            like_float,
            like_map,
            like_map,
            shape(seqs, pairs, block_len, 4),
            shape(seqs, pairs, 2, block_len),
        ],
        scratch_shapes=[pltpu.VMEM((block_len, block_len), F32)] * 2,
        compiler_params=vmem(32),
    )(grad_scan, values, write_map, read_map, incoming, col_pack, row_pack, skip_row)

    spread_out, *early_got = lax.optimization_barrier((spread_out, *early_got, grad_values))[:3]
    outgoing = swap(scanned(spread_out, spread_in, width, True, BACK_OUT), "seq")
    early_acc = summing.across(*summing.keep(*early, early_got))
    outgoing, early_acc = lax.optimization_barrier((outgoing, early_acc))
    outgoing = from_shares(outgoing, seqs * pairs)
    rest = summing.rest
    if rest:
        early_acc = summing.halved(early_acc, rest[0])

    rows6 = pl.BlockSpec((1, 6, LANES), lambda s, j: (s, 0, j))
    grad_value_pre, tail_part, head_part, value_rows, grad_write, grad_end = pl.pallas_call(
        partial(state_back_kernel, head_size),
        grid=grid,
        in_specs=[
            pair, pair, wide, shared, cols8, wide, shared, wide, prior, taps4, lane_row, valids,
        ],
        out_specs=[
            wide, prior, prior, rows6, shared,
            pl.BlockSpec((1, 1, block_len, 2), lambda s, j: (s, j, 0, 0)),
        ],
        out_shape=[
            like_values,
            shape(seqs, PAD, inner),
            shape(seqs, PAD, inner),
            shape(seqs, 6, inner),
            like_map,
            shape(seqs, pairs, block_len, 2),
        ],
        compiler_params=vmem(32),
    )(
        outgoing, incoming, values, write_map, col_pack, grad_values, grad_write,
        value_pre, value_prior, conv_value, bias_row, valid,
    )

    early_acc, grad_value_pre = lax.optimization_barrier((early_acc, grad_value_pre))
    for mask in rest[1:]:
        early_acc = summing.halved(early_acc, mask)
    early_acc = early_acc.astype(BF16)

    handed = jnp.where(core == 0, grad_read, grad_write)
    own_maps = jnp.where(core == 0, grad_write, grad_read)
    grad_maps = own_maps + lax.ppermute(handed, "head", [(0, 1), (1, 0)])
    maps_gext, grad_conv_maps, grad_maps_bias = maps_back(grad_maps)

    reach = kernel_len - 1
    halo = jnp.concatenate([head_part[:, PAD - reach :], maps_gext[:, :reach]], axis=-1)
    from_next = passed_along(halo, "seq", -1) * tail_keep
    tail_value = tail_part[:, PAD - reach :] + from_next[..., :inner]
    grad_value_pre = lax.dynamic_update_slice_in_dim(
        grad_value_pre, tail_value.astype(BF16), block_len - reach, 1
    )
    maps_gown = maps_gext[:, reach:]
    maps_gown = maps_gown.at[:, block_len - reach :].add(from_next[..., inner:])
    grad_maps_pre = maps_gown.astype(BF16)

    def unpaired(a):
        return jnp.transpose(a, (0, 2, 1, 3)).reshape(seqs, block_len, heads)

    gend = unpaired(grad_end)
    from_row = unpaired(jnp.swapaxes(drow, 2, 3))
    gentry = unpaired(dcol[..., 2:])
    gcarry = jnp.sum(value_rows[:, 5].reshape(seqs, heads, head_size), axis=-1)
    ended = gend * end_weight
    grad_cum = unpaired(dcol[..., :2]) - from_row * step_size - ended + gentry * entry_decay
    at_last = jnp.sum(ended, axis=1) + gcarry * carry_decay
    grad_cum = grad_cum.at[:, -1].add(at_last)
    grad_rate = jnp.einsum("tq,sth->sqh", tril, grad_cum, precision=HIGHEST)
    grad_size = from_row + gend * end_plain + grad_rate * decay_rate
    grad_step = grad_size * jax.nn.sigmoid(step_pre)
    grad_decay_log = jnp.sum(grad_rate * step_size, axis=(0, 1)) * decay_rate
    grad_step_pre = grad_step.astype(BF16)
    grad_step_bias = jnp.sum(grad_step, axis=(0, 1))

    narrow = jnp.concatenate([grad_maps_pre, grad_step_pre], axis=-1)
    narrow = jnp.pad(narrow, ((0, 0), (0, 0), (0, -narrow.shape[-1] % LANES)))
    right = flat(jnp.concatenate([grad_value_pre, narrow], axis=-1))
    half = model_width // 2
    late = product(normed_flat[:, :half], right), product(normed_flat[:, half:], right)
    early_acc, *late = (early_acc, *late)
    late_got = summing.send(*late)
    backward = list(reversed(rest))
    for mask in backward[:1]:
        early_acc = summing.grown(early_acc, mask)

    def pulled_back(rows_of):
        grads = (grad_gate_pre, proj_gate), (grad_value_pre, proj_value)
        grads += (grad_maps_pre, proj_maps), (grad_step_pre, proj_step)
        total = None
        for grad, weight in grads:
            part = jnp.einsum("sqk,dk->sqd", grad, rows_of(weight), preferred_element_type=F32)
            total = part if total is None else total + part
        return total

    def features(array, which, axis):
        return lax.dynamic_slice_in_dim(array, which * half_width, half_width, axis)

    weighing = gain_full * residual
    to_other = pulled_back(lambda w: features(w, 1 - core, 0))
    from_other = lax.ppermute(to_other, "head", [(0, 1), (1, 0)])
    mine = pulled_back(lambda w: features(w, core, 0))
    row_part = jnp.sum(to_other * features(weighing, 1 - core, 2), axis=-1, keepdims=True)
    row_part = row_part + jnp.sum(mine * features(weighing, core, 2), axis=-1, keepdims=True)
    row_sum = lax.psum(row_part, "head")
    grad_in_loc = mine + from_other

    early_acc, *late_got = lax.optimization_barrier((early_acc, *late_got, row_sum))[:3]
    late_acc = summing.keep(*late, late_got)
    late_acc = summing.across(*late_acc)
    for mask in backward[1:]:
        early_acc = summing.grown(early_acc, mask)
    hidden_loc = hidden_in.astype(F32)
    grad_norm_gain = jnp.sum(grad_in_loc * hidden_loc * inv_norm, axis=(0, 1))
    grad_normal = grad_in_loc * norm_gain.astype(F32)
    input_grad = (
        out_grad.astype(F32)
        + inv_norm * grad_normal
        - hidden_loc * (inv_norm * inv_norm * inv_norm) * (row_sum / model_width)
    )

    early_acc, late_acc, input_grad = lax.optimization_barrier((early_acc, late_acc, input_grad))
    for mask in rest[:1]:
        late_acc = summing.halved(late_acc, mask)
    early_parts = summing.split(early_acc)

    normed_out = after(normed_out, early_acc)
    to_other = project(normed_out, features(proj_out, 1 - core, 1))
    from_other = lax.ppermute(to_other, "head", [(0, 1), (1, 0)])
    branch = project(normed_out, features(proj_out, core, 1)) + from_other
    mixed_out = (hidden_loc + branch).astype(BF16)

    late_acc, part_a, part_b, mixed_out = lax.optimization_barrier(
        (late_acc, *early_parts, mixed_out)
    )
    for mask in rest[1:]:
        late_acc = summing.halved(late_acc, mask)
    late_acc = late_acc.astype(BF16)
    sum_out, sum_gate = summing.whole(part_a, part_b)

    late_acc, sum_out, sum_gate = lax.optimization_barrier((late_acc, sum_out, sum_gate))
    for mask in backward:
        late_acc = summing.grown(late_acc, mask)
    grad_proj_out, grad_proj_gate = sum_out.astype(F32), sum_gate.astype(F32)
    sum_a, sum_b = summing.whole(*summing.split(late_acc))
    maps_end = inner + proj_maps.shape[1]

    def cut(start, stop):
        return jnp.concatenate([sum_a[:, start:stop], sum_b[:, start:stop]], axis=0).astype(F32)

    grad_proj_value = cut(0, inner)
    grad_proj_maps = cut(inner, maps_end)
    grad_proj_step = cut(maps_end, maps_end + heads)

    gate_rows = jnp.sum(gate_rows, axis=0)
    value_rows = jnp.sum(value_rows, axis=0)
    grad_gate_gain = gate_rows[0]
    grad_skip = jnp.sum(gate_rows[1].reshape(heads, head_size), axis=1)
    smalls = [
        grad_norm_gain,
        value_rows[:kernel_len],
        value_rows[kernel_len],
        grad_conv_maps,
        grad_maps_bias,
        grad_step_bias,
        grad_decay_log,
        grad_skip,
        grad_gate_gain,
    ]
    line = jnp.concatenate([a.reshape(-1) for a in smalls])
    line = jnp.pad(line, (0, -line.shape[0] % (8 * LANES))).reshape(-1, LANES)
    line = sum_small(line, "seq").reshape(-1)
    found, start = [], 0
    for a in smalls:
        found.append(line[start : start + a.size].reshape(a.shape))
        start += a.size
    (
        grad_norm_gain,
        grad_conv_value,
        grad_value_bias,
        grad_conv_maps,
        grad_maps_bias,
        grad_step_bias,
        grad_decay_log,
        grad_skip,
        grad_gate_gain,
    ) = found
    return (
        mixed_out,
        input_grad,
        grad_norm_gain,
        grad_proj_gate,
        grad_proj_value,
        grad_proj_maps,
        grad_proj_step,
        grad_conv_value,
        grad_value_bias,
        grad_conv_maps,
        grad_maps_bias,
        grad_step_bias,
        grad_decay_log,
        grad_skip,
        grad_gate_gain,
        grad_proj_out,
    )


def solution(mesh):
    placed = (
        P(None, "seq", "head"),
        P(None, "seq"),
        P("head"),
        P(None, "head"),
        P(None, "head"),
        P(None, "head"),
        P(None, "head"),
        P(None, "head"),
        P("head"),
        P(None, "head"),
        P("head"),
        P("head"),
        P("head"),
        P("head"),
        P("head"),
        P("head", None),
        P(None, "seq", "head"),
    )
    return jax.shard_map(
        shards,
        mesh=mesh,
        in_specs=placed,
        out_specs=(
            P(None, "seq", "head"),
            P(None, "seq", "head"),
            P("head"),
            P(None, "head"),
            P(None, "head"),
            P(None, "head"),
            P(None, "head"),
            P(None, "head"),
            P("head"),
            P(None, "head"),
            P("head"),
            P("head"),
            P("head"),
            P("head"),
            P("head"),
            P("head", None),
        ),
        check_vma=False,
    )
```

```python
from functools import partial

import jax
import jax.numpy as jnp
from jax import lax
from jax.experimental import pallas as pl
from jax.experimental.pallas import tpu as pltpu
from jax.sharding import PartitionSpec as P

EPS = 1e-05
HIGHEST = lax.Precision.HIGHEST
F32 = jnp.float32
BF16 = jnp.bfloat16
LANES = 128
PAD = 16
NEVER = -1e30
EXTRA = 8


def passed_along(shard, axis, by):
    peers = lax.axis_size(axis)
    pairs = [(i, i + by) for i in range(peers) if 0 <= i + by < peers]
    return lax.ppermute(shard, axis, pairs)


def flip(shard, axis, mask):
    count = lax.axis_size(axis)
    return lax.ppermute(shard, axis, [(i, i ^ mask) for i in range(count)])


def dot(a, b, ca=1, cb=0):
    return lax.dot_general(a, b, (((ca,), (cb,)), ((), ())), preferred_element_type=F32)


def halves(a):
    high = a.astype(BF16)
    return high, (a - high.astype(F32)).astype(BF16)


def dot_wide(a, b, ca=1, cb=0):
    high, low = halves(a)
    return dot(high, b, ca, cb) + dot(low, b, ca, cb)


def dot_right(a, b, ca=1, cb=0):
    if b.dtype == BF16:
        return dot(a, b, ca, cb)
    high, low = halves(b)
    return dot(a, high, ca, cb) + dot(a, low, ca, cb)


def dot_both(a, b, ca=1, cb=0):
    if b.dtype == BF16:
        return dot_wide(a, b, ca, cb)
    high, low = halves(b)
    return dot_wide(a, high, ca, cb) + dot(a.astype(BF16), low, ca, cb)


def silu_slope(source):
    sigmoid = jax.nn.sigmoid(source)
    return sigmoid * (1.0 + source * (1.0 - sigmoid))


def exact(a, b, ca=1, cb=0):
    return lax.dot_general(
        a, b, (((ca,), (cb,)), ((), ())), precision=HIGHEST, preferred_element_type=F32
    )


def triangle(size):
    later = lax.broadcasted_iota(jnp.int32, (size, size), 0)
    earlier = lax.broadcasted_iota(jnp.int32, (size, size), 1)
    return (later >= earlier).astype(F32), (later == earlier).astype(F32)


def spread_heads(heads, lanes):
    head = lax.broadcasted_iota(jnp.int32, (heads, lanes), 0)
    lane = lax.broadcasted_iota(jnp.int32, (heads, lanes), 1)
    return (lane // (lanes // heads) == head).astype(F32)


def decay_terms(pre, rate, seg, tril):
    step = jnp.maximum(pre, 0.0) + jnp.log1p(jnp.exp(-jnp.abs(pre)))
    cum = exact(tril, step * rate)
    last = cum[cum.shape[0] - 1 :]
    seg_last = seg[seg.shape[0] - 1 :]
    fresh = (seg == 0).astype(F32)
    end_plain = jnp.exp(last - cum) * (seg == seg_last).astype(F32)
    carry = jnp.exp(last) * (seg_last == 0).astype(F32)
    return step, cum, end_plain, jnp.exp(cum) * fresh, carry


def pack_kernel(groups, pairs, pre_ref, log_ref, seg_ref, col_ref, row_ref, decay_ref):
    pre, seg = pre_ref[0], seg_ref[0]
    block_len, heads = pre.shape
    per = heads // groups
    tril, eye = triangle(block_len)
    step, cum, end_plain, entry, carry = decay_terms(pre, -jnp.exp(log_ref[...]), seg, tril)
    end = end_plain * step
    segs = jnp.broadcast_to(seg, (block_len, per))
    turned = exact(jnp.concatenate([cum, step, segs], axis=1), eye, 0, 0)
    for g in range(groups):
        part = slice(g * per, (g + 1) * per)
        col_ref[0, g] = jnp.concatenate([cum[:, part], end[:, part], entry[:, part], segs], axis=1)
        row_ref[0, g] = jnp.concatenate(
            [turned[part], turned[heads + g * per : heads + (g + 1) * per], turned[2 * heads :]],
            axis=0,
        )
    lanes = exact(carry, spread_heads(heads, pairs * LANES))
    for j in range(pairs):
        decay_ref[j] = jnp.broadcast_to(lanes[:, j * LANES : (j + 1) * LANES], decay_ref.shape[1:])


def unpack_kernel(groups, pre_ref, log_ref, seg_ref, dcol_ref, drow_ref, gend_ref, rows_ref, out_ref, sums_ref):
    pre, seg = pre_ref[0], seg_ref[0]
    block_len, heads = pre.shape
    per = heads // groups
    tril, eye = triangle(block_len)
    rate = -jnp.exp(log_ref[...])
    step, cum, end_plain, entry, carry = decay_terms(pre, rate, seg, tril)
    dcum = jnp.concatenate([dcol_ref[0, g, :, :per] for g in range(groups)], axis=1)
    gentry = jnp.concatenate([dcol_ref[0, g, :, per:] for g in range(groups)], axis=1)
    gend = jnp.concatenate([gend_ref[0, g] for g in range(groups)], axis=1)
    from_row = exact(
        eye, jnp.concatenate([drow_ref[0, g] for g in range(groups)], axis=0), 1, 1
    )
    gcarry = rows_ref[0, rows_ref.shape[1] - 1 :]
    gcarry = exact(gcarry, spread_heads(heads, gcarry.shape[1]), 1, 1)
    ended = gend * (end_plain * step)
    at_last = jnp.sum(ended, axis=0, keepdims=True) + gcarry * carry
    grad_cum = dcum - from_row * step - ended + gentry * entry
    grad_rate = exact(tril, grad_cum, 0, 0) + at_last
    grad_step = (from_row + gend * end_plain + grad_rate * rate) * jax.nn.sigmoid(pre)
    out_ref[0] = grad_step.astype(BF16)
    by_log = jnp.sum(grad_rate * step, axis=0, keepdims=True) * rate
    sums_ref[0] = jnp.concatenate([jnp.sum(grad_step, axis=0, keepdims=True), by_log], axis=0)


def shifted(pre_ref, prior_ref):
    ext = jnp.concatenate([prior_ref[0].astype(F32), pre_ref[0].astype(F32)], axis=0)
    block_len = pre_ref.shape[1]
    return [ext[PAD - 3 + i : PAD - 3 + i + block_len] for i in range(4)]


def convolved(taps, kernel_ref, bias_ref, valid):
    summed = bias_ref[...]
    for i in range(4):
        summed = summed + kernel_ref[i : i + 1, :] * taps[i] * valid[:, i : i + 1]
    return summed


def column(col_ref, kind, a, per):
    return col_ref[0, 0, :, kind * per + a : kind * per + a + 1]


def by_head(col_ref, kind, per, head_size):
    lane = lax.broadcasted_iota(jnp.int32, (1, 2 * head_size), 1)
    parts = [
        jnp.where(lane < head_size, column(col_ref, kind, a, per), column(col_ref, kind, a + 1, per))
        for a in range(0, per, 2)
    ]
    return jnp.concatenate(parts, axis=1)


def head_parts(per, head_size):
    return [slice(a * head_size, (a + 1) * head_size) for a in range(per)]


def side(ref):
    return jnp.concatenate([ref[j] for j in range(ref.shape[0])], axis=1)


def local_kernel(per, head_size, pre_ref, prior_ref, kernel_ref, bias_ref, valid_ref, write_ref, col_ref, decay_ref, values_ref, state_ref):
    taps = shifted(pre_ref, prior_ref)
    summed = convolved(taps, kernel_ref, bias_ref, valid_ref[0])
    values = (summed * jax.nn.sigmoid(summed)).astype(BF16)
    values_ref[0] = values
    write = write_ref[0].astype(F32)
    width = write.shape[1]
    states = []
    for a, part in enumerate(head_parts(per, head_size)):
        weighted = (column(col_ref, 1, a, per) * write).astype(BF16)
        states.append(dot(weighted, values[:, part], 0, 0))
    for j in range(per // 2):
        state_ref[j, :width] = jnp.concatenate(states[2 * j : 2 * j + 2], axis=1)
        state_ref[j, width:] = decay_ref[j]


def kept_mask(seg_col, seg_row):
    block_len = seg_col.shape[0]
    later = lax.broadcasted_iota(jnp.int32, (block_len, block_len), 0)
    earlier = lax.broadcasted_iota(jnp.int32, (block_len, block_len), 1)
    return (later >= earlier) & (seg_col == seg_row)


def diag_kernel(per, head_size, values_ref, write_ref, read_ref, col_ref, row_ref, skip_ref, out_ref):
    scores = dot(read_ref[0], write_ref[0], 1, 1)
    keep = kept_mask(column(col_ref, 3, 0, per), row_ref[0, 0, 2 * per : 2 * per + 1, :])
    values = values_ref[0]
    outs = []
    for a, part in enumerate(head_parts(per, head_size)):
        spread = column(col_ref, 0, a, per) - row_ref[0, 0, a : a + 1, :]
        decay = jnp.exp(jnp.where(keep, spread, NEVER))
        mixing = (decay * scores * row_ref[0, 0, per + a : per + a + 1, :]).astype(BF16)
        outs.append(dot(mixing, values[:, part]))
    out_ref[0] = jnp.concatenate(outs, axis=1) + skip_ref[...] * values.astype(F32)


def gate_kernel(per, head_size, diag_ref, read_ref, inc_ref, col_ref, gate_ref, back_ref, gain_ref, scan_ref, sums_ref):
    carried = dot_right(read_ref[0], side(inc_ref))
    scan = diag_ref[0] + by_head(col_ref, 2, per, head_size) * carried
    scan_ref[0] = scan
    gate = gate_ref[0]
    prod = scan * (gate * jax.nn.sigmoid(gate))
    square = jnp.sum(prod * prod, axis=1, keepdims=True)
    inner = jnp.sum(back_ref[0] * gain_ref[...] * prod, axis=1, keepdims=True)
    both = jnp.concatenate([square, inner], axis=1)
    both = exact(both, triangle(both.shape[0])[1], 0, 0)

    @pl.when(pl.program_id(1) == 0)
    def _():
        sums_ref[0] = both

    @pl.when(pl.program_id(1) > 0)
    def _():
        sums_ref[0] += both


def back_kernel(per, head_size, inner_all, scan_ref, gate_ref, back_ref, gain_ref, sums_ref, values_ref, read_ref, col_ref, normed_ref, gscan_ref, ggate_ref, state_ref, rows_ref):
    sums = exact(triangle(sums_ref.shape[2])[1], sums_ref[0], 1, 1)
    inv = lax.rsqrt(sums[:, 0:1] / inner_all + EPS)
    inner = sums[:, 1:2] / inner_all
    scan, gate, back = scan_ref[0], gate_ref[0], back_ref[0]
    gain = gain_ref[...]
    sigmoid = jax.nn.sigmoid(gate)
    act = gate * sigmoid
    prod = scan * act
    gated_norm = prod * inv
    normed_ref[0] = (gated_norm * gain).astype(BF16)
    grad = inv * (back * gain) - prod * (inv * inv * inv * inner)
    gscan = (grad * act).astype(BF16)
    gscan_ref[0] = gscan
    ggate_ref[0] = (grad * scan * (sigmoid * (1.0 + gate * (1.0 - sigmoid)))).astype(BF16)
    gscan = gscan.astype(F32)
    gain_row = jnp.sum(back * gated_norm, axis=0, keepdims=True)
    skip_row = jnp.sum(gscan * values_ref[0].astype(F32), axis=0, keepdims=True)
    rows_ref[0] = jnp.concatenate([gain_row, skip_row], axis=0)
    entry = by_head(col_ref, 2, per, head_size) * gscan
    high, low = halves(entry)
    state = dot(read_ref[0], high, 0, 0) + dot(read_ref[0], low, 0, 0)
    for j in range(per // 2):
        state_ref[j] = state[:, j * LANES : (j + 1) * LANES]


def mix_back_kernel(per, head_size, gscan_ref, values_ref, write_ref, read_ref, inc_ref, col_ref, row_ref, skip_ref, gvalues_ref, gread_ref, gwrite_ref, dcol_ref, drow_ref, gscores_ref):
    turn = pl.program_id(1)
    scores = dot(read_ref[0], write_ref[0], 1, 1)
    keep = kept_mask(column(col_ref, 3, 0, per), row_ref[0, 0, 2 * per : 2 * per + 1, :])
    values, gscan = values_ref[0], gscan_ref[0]
    gscan_f = gscan.astype(F32)
    parts, cols, rows, total = [], [], [], None
    for a, part in enumerate(head_parts(per, head_size)):
        step = row_ref[0, 0, per + a : per + a + 1, :]
        spread = column(col_ref, 0, a, per) - row_ref[0, 0, a : a + 1, :]
        decay = jnp.exp(jnp.where(keep, spread, NEVER))
        mixing = (decay * scores * step).astype(BF16)
        parts.append(dot(mixing, gscan[:, part], 0, 0))
        pulled = dot(gscan[:, part], values[:, part], 1, 1) * decay
        stepped = pulled * step
        total = stepped if total is None else total + stepped
        cols.append(jnp.sum(stepped * scores, axis=1, keepdims=True))
        rows.append(jnp.sum(pulled * scores, axis=0, keepdims=True))
    gvalues_ref[0] = skip_ref[...] * gscan_f + jnp.concatenate(parts, axis=1)
    incoming = side(inc_ref)
    entered = gscan_f * dot_right(read_ref[0], incoming)
    entry = by_head(col_ref, 2, per, head_size) * gscan_f
    gread = dot_both(entry, incoming, 1, 1)
    for part in head_parts(per, head_size):
        cols.append(jnp.sum(entered[:, part], axis=1, keepdims=True))
    dcol_ref[0, 0] = jnp.concatenate(cols, axis=1)
    drow_ref[0, 0] = jnp.concatenate(rows, axis=0)

    @pl.when(turn == 0)
    def _():
        gread_ref[0] = gread
        gscores_ref[...] = total

    @pl.when(turn > 0)
    def _():
        gread_ref[0] += gread
        gscores_ref[...] += total

    @pl.when(turn == pl.num_programs(1) - 1)
    def _():
        gread_ref[0] += dot_wide(gscores_ref[...], write_ref[0])
        gwrite_ref[0] = dot_wide(gscores_ref[...], read_ref[0], 0, 0)


def state_back_kernel(per, head_size, out_ref, inc_ref, values_ref, write_ref, col_ref, gpart_ref, gwpart_ref, pre_ref, prior_ref, kernel_ref, bias_ref, valid_ref, gpre_ref, tail_ref, head_ref, rows_ref, gwrite_ref, gend_ref):
    turn = pl.program_id(1)
    outgoing = side(out_ref)
    out_high, out_low = halves(outgoing)
    values = values_ref[0]
    write = write_ref[0].astype(F32)
    parts, ends, total = [], [], None
    for a, part in enumerate(head_parts(per, head_size)):
        end = column(col_ref, 1, a, per)
        weighted = (end * write).astype(BF16)
        high, low = out_high[:, part], out_low[:, part]
        parts.append(dot(weighted, high) + dot(weighted, low))
        gweighted = dot(values[:, part], high, 1, 1) + dot(values[:, part], low, 1, 1)
        ends.append(jnp.sum(gweighted * write, axis=1, keepdims=True))
        total = gweighted * end if total is None else total + gweighted * end
    gend_ref[0, 0] = jnp.concatenate(ends, axis=1)

    @pl.when(turn == 0)
    def _():
        gwrite_ref[0] = gwpart_ref[0] + total

    @pl.when(turn > 0)
    def _():
        gwrite_ref[0] += total

    gvalues = gpart_ref[0] + jnp.concatenate(parts, axis=1)
    taps = shifted(pre_ref, prior_ref)
    valid = valid_ref[0]
    source = convolved(taps, kernel_ref, bias_ref, valid)
    grad = gvalues * silu_slope(source)
    block_len = grad.shape[0]
    blank = jnp.zeros((PAD, grad.shape[1]), F32)
    rows, summed = [], None
    for i in range(4):
        held = grad * valid[:, i : i + 1]
        rows.append(jnp.sum(held * taps[i], axis=0, keepdims=True))
        padded = jnp.concatenate([blank, kernel_ref[i : i + 1, :] * held, blank], axis=0)
        moved = padded[3 - i : 3 - i + block_len + PAD]
        summed = moved if summed is None else summed + moved
    rows.append(jnp.sum(grad, axis=0, keepdims=True))
    rows.append(jnp.sum(outgoing * side(inc_ref), axis=0, keepdims=True))
    rows_ref[0] = jnp.concatenate(rows, axis=0)
    head_ref[0] = summed[:PAD]
    own = summed[PAD:]
    gpre_ref[0] = own.astype(BF16)
    tail_ref[0] = own[block_len - PAD :]


def scan_kernel(reverse, width, states_ref, decay_ref, out_ref):
    count = states_ref.shape[0]

    def one(turn, carried):
        block = count - 1 - turn if reverse else turn
        out_ref[pl.ds(block, 1)] = carried[None]
        decay = decay_ref[pl.ds(block, 1)][0, width : width + 1]
        return decay * carried + states_ref[pl.ds(block, 1)][0, :width]

    lax.fori_loop(0, count, one, jnp.zeros(out_ref.shape[1:], F32))


def vmem(mib):
    return pltpu.CompilerParams(vmem_limit_bytes=mib << 20)


def scanned(states, decays, width, reverse):
    count, _, share = states.shape
    return pl.pallas_call(
        partial(scan_kernel, reverse, width),
        out_shape=jax.ShapeDtypeStruct((count, width, share), F32),
        compiler_params=vmem(60),
    )(states, decays)


def to_shares(rows, count):
    pairs, width, lanes = rows.shape
    if pairs == count:
        return rows
    cut = count // pairs
    split = rows.reshape(pairs, width, cut, lanes // cut)
    return jnp.transpose(split, (0, 2, 1, 3)).reshape(count, width, lanes // cut)


def from_shares(shares, pairs):
    count, width, share = shares.shape
    if pairs == count:
        return shares
    cut = count // pairs
    split = shares.reshape(pairs, cut, width, share)
    return jnp.transpose(split, (0, 2, 1, 3)).reshape(pairs, width, cut * share)


def swap(shares, axis):
    return lax.all_to_all(shares, axis, 0, 0, tiled=True)


def ordered(own, got, bit):
    return jnp.where(
        bit == 0, jnp.concatenate([own, got], axis=0), jnp.concatenate([got, own], axis=0)
    )


class Summing:
    def __init__(self, axis):
        self.axis = axis
        count = lax.axis_size(axis)
        self.place = lax.axis_index(axis)
        self.rest = [1 << b for b in range(2, count.bit_length() - 1)]

    def bit(self, mask):
        return (self.place & mask) // mask

    def halved(self, acc, mask, rider=None):
        piece = acc.shape[0] // 2
        bit = self.bit(mask)
        sent = lax.dynamic_slice_in_dim(acc, (1 - bit) * piece, piece, 0)
        kept = lax.dynamic_slice_in_dim(acc, bit * piece, piece, 0)
        if rider is None:
            return kept + flip(sent, self.axis, mask)
        got = flip(jnp.concatenate([sent, rider], axis=0), self.axis, mask)
        return kept + got[:piece], rider + got[piece:]

    def parts(self, product_a, product_b):
        bit_a, bit_b = self.bit(1), self.bit(2)
        sent = product_a(1 - bit_a).astype(BF16), product_b(1 - bit_b).astype(BF16)
        return sent, (product_a(bit_a), product_b(bit_b))

    def traded(self, sent):
        return flip(sent[0], self.axis, 1), flip(sent[1], self.axis, 2)

    def across(self, kept, got):
        acc_a, acc_b = [own + other.astype(F32) for own, other in zip(kept, got)]
        return jnp.concatenate([self.halved_low(acc_a, 2), self.halved_low(acc_b, 1)], axis=0)

    def halved_low(self, acc, mask):
        piece = acc.shape[0] // 2
        bit = self.bit(mask)
        sent = lax.dynamic_slice_in_dim(acc, (1 - bit) * piece, piece, 0)
        kept = lax.dynamic_slice_in_dim(acc, bit * piece, piece, 0)
        return kept + flip(sent.astype(BF16), self.axis, mask).astype(F32)

    def grown(self, own, mask, rider=None):
        if rider is None:
            return ordered(own, flip(own, self.axis, mask), self.bit(mask))
        parts, rest = [], rider
        for _ in range(3):
            high = lax.reduce_precision(rest, 8, 7)
            parts.append(high.astype(BF16))
            rest = rest - high
        size = own.shape[0]
        got = flip(jnp.concatenate([own, *parts], axis=0), self.axis, mask)
        extra = got[size:].astype(F32).reshape(3, *rider.shape)
        return ordered(own, got[:size], self.bit(mask)), rider + (extra[0] + extra[1] + extra[2])

    def split(self, acc, rider=None):
        half = acc.shape[0] // 2
        return self.grown(acc[:half], 2, rider), self.grown(acc[half:], 1)

    def whole(self, part_a, part_b, rider=None):
        return self.grown(part_a, 1, rider), self.grown(part_b, 2)


def together(core, own):
    other = lax.ppermute(own, "head", [(0, 1), (1, 0)])
    return jnp.where(
        core == 0,
        jnp.concatenate([own, other], axis=-1),
        jnp.concatenate([other, own], axis=-1),
    )


def after(array, *others):
    return lax.optimization_barrier((array, *others))[0]


def columns(array, start, size):
    return lax.dynamic_slice_in_dim(array, start, size, 1)


def shards(
    hidden_in,
    doc_start,
    norm_gain,
    proj_gate,
    proj_value,
    proj_maps,
    proj_step,
    conv_value,
    value_bias,
    conv_maps,
    maps_bias,
    step_bias,
    decay_log,
    skip_gain,
    gate_gain,
    proj_out,
    out_grad,
):
    core = lax.axis_index("head")
    count = lax.axis_size("seq")
    seqs, block_len, half_width = hidden_in.shape
    inner = proj_value.shape[1]
    heads = proj_step.shape[1]
    head_size = inner // heads
    kernel_len = conv_value.shape[0]
    head_devices = lax.axis_size("head")
    inner_all = inner * head_devices
    model_width = half_width * head_devices
    width = proj_maps.shape[1] * head_devices // 2
    pairs = inner // LANES
    tokens = seqs * block_len

    hidden_full = together(core, hidden_in)
    gain_full = lax.all_gather(norm_gain, "head", axis=0, tiled=True).astype(F32)

    tril = jnp.tril(jnp.ones((block_len, block_len), F32))
    segment = jnp.round(jnp.einsum("tq,sq->st", tril, doc_start.astype(F32), precision=HIGHEST))
    tail_starts = doc_start[:, block_len - (kernel_len - 1) :]
    after_tail = jnp.cumsum(tail_starts[:, ::-1], axis=1)[:, ::-1] - tail_starts
    tail_keep = (after_tail == 0).astype(F32)[..., None]
    tail_rows = hidden_full[:, block_len - (kernel_len - 1) :] * tail_keep.astype(BF16)
    prior_hidden = passed_along(tail_rows, "seq", 1)
    prior_hidden = jnp.pad(prior_hidden, ((0, 0), (PAD - (kernel_len - 1), 0), (0, 0)))
    segment_ext = jnp.concatenate([jnp.zeros((seqs, kernel_len - 1), F32), segment], axis=1)
    valid = jnp.stack(
        [segment_ext[:, i : i + block_len] == segment for i in range(kernel_len)], axis=-1
    ).astype(F32)

    def normalize(rows):
        residual = rows.astype(F32)
        inv = lax.rsqrt(jnp.mean(residual * residual, axis=-1, keepdims=True) + EPS)
        return residual, inv, (residual * inv * gain_full).astype(BF16)

    residual, inv_norm, normed = normalize(hidden_full)
    normed_prior = normalize(prior_hidden)[2]

    def project(rows, weight):
        return jnp.dot(rows, weight, preferred_element_type=F32)

    maps_pre = project(normed, proj_maps).astype(BF16)
    maps_prior = project(normed_prior, proj_maps).astype(BF16)
    step_pre = project(normed, proj_step) + step_bias
    value_pre = project(normed, proj_value).astype(BF16)
    value_prior = project(normed_prior, proj_value).astype(BF16)

    def convolve(extended, kernel, bias):
        summed = bias
        for i in range(kernel_len):
            summed = summed + kernel[i] * extended[:, i : i + block_len] * valid[..., i : i + 1]
        return jax.nn.silu(summed)

    maps_ext = jnp.concatenate(
        [maps_prior[:, PAD - (kernel_len - 1) :], maps_pre], axis=1
    ).astype(F32)
    maps_act, maps_back = jax.vjp(convolve, maps_ext, conv_maps, maps_bias)
    maps_all = lax.all_gather(maps_act.astype(BF16), "head", axis=2, tiled=True)
    write_map, read_map = maps_all[..., :width], maps_all[..., width:]

    groups = 2 if pairs % 2 == 0 else 1
    cut = pairs // groups
    per = heads // groups
    seg_col = segment[..., None]
    log_row = decay_log[None]
    each = pl.BlockSpec((1, block_len, heads), lambda s: (s, 0, 0))
    whole_row = pl.BlockSpec((1, heads), lambda s: (0, 0))
    one_col = pl.BlockSpec((1, block_len, 1), lambda s: (s, 0, 0))
    col_pack, row_pack, decay_rows = pl.pallas_call(
        partial(pack_kernel, groups, pairs),
        grid=(seqs,),
        in_specs=[each, whole_row, one_col],
        out_specs=[
            pl.BlockSpec((1, groups, block_len, 4 * per), lambda s: (s, 0, 0, 0)),
            pl.BlockSpec((1, groups, 3 * per, block_len), lambda s: (s, 0, 0, 0)),
            pl.BlockSpec((pairs, EXTRA, LANES), lambda s: (s, 0, 0)),
        ],
        out_shape=[
            jax.ShapeDtypeStruct((seqs, groups, block_len, 4 * per), F32),
            jax.ShapeDtypeStruct((seqs, groups, 3 * per, block_len), F32),
            jax.ShapeDtypeStruct((seqs * pairs, EXTRA, LANES), F32),
        ],
        compiler_params=vmem(60),
    )(step_pre, log_row, seg_col)
    skip_row = jnp.repeat(skip_gain, head_size)[None]
    bias_row = value_bias[None]
    gain_row = gate_gain[None]

    grid = (seqs, groups)
    lanes = cut * LANES
    wide = pl.BlockSpec((1, block_len, lanes), lambda s, g: (s, 0, g))
    prior = pl.BlockSpec((1, PAD, lanes), lambda s, g: (s, 0, g))
    shared = pl.BlockSpec((1, block_len, width), lambda s, g: (s, 0, 0))
    taps4 = pl.BlockSpec((kernel_len, lanes), lambda s, g: (0, g))
    lane_row = pl.BlockSpec((1, lanes), lambda s, g: (0, g))
    valids = pl.BlockSpec((1, block_len, kernel_len), lambda s, g: (s, 0, 0))
    cols = pl.BlockSpec((1, 1, block_len, 4 * per), lambda s, g: (s, g, 0, 0))
    rows = pl.BlockSpec((1, 1, 3 * per, block_len), lambda s, g: (s, g, 0, 0))
    pair = pl.BlockSpec((cut, width, LANES), lambda s, g: (s * groups + g, 0, 0))
    pair_ext = pl.BlockSpec((cut, width + EXTRA, LANES), lambda s, g: (s * groups + g, 0, 0))
    pair_tail = pl.BlockSpec((cut, EXTRA, LANES), lambda s, g: (s * groups + g, 0, 0))
    two = pl.BlockSpec((1, 2, block_len), lambda s, g: (s, 0, 0))

    def shape(*dims, dtype=F32):
        return jax.ShapeDtypeStruct(dims, dtype)

    like_values = shape(seqs, block_len, inner, dtype=BF16)
    like_float = shape(seqs, block_len, inner)
    like_states = shape(seqs * pairs, width, LANES)
    like_map = shape(seqs, block_len, width)

    values, payload = pl.pallas_call(
        partial(local_kernel, per, head_size),
        grid=grid,
        in_specs=[wide, prior, taps4, lane_row, valids, shared, cols, pair_tail],
        out_specs=[wide, pair_ext],
        out_shape=[like_values, shape(seqs * pairs, width + EXTRA, LANES)],
        compiler_params=vmem(60),
    )(value_pre, value_prior, conv_value, bias_row, valid, write_map, col_pack, decay_rows)

    spread_in = swap(to_shares(payload, count), "seq")

    gate_pre = project(normed, proj_gate)
    grad_full = together(core, out_grad)
    grad_normed = jnp.einsum("sqd,id->sqi", grad_full, proj_out, preferred_element_type=F32)
    diag = pl.pallas_call(
        partial(diag_kernel, per, head_size),
        grid=grid,
        in_specs=[wide, shared, shared, cols, rows, lane_row],
        out_specs=wide,
        out_shape=like_float,
        compiler_params=vmem(60),
    )(values, write_map, read_map, col_pack, row_pack, skip_row)

    spread_in = after(spread_in, gate_pre, grad_normed, row_pack)
    incoming = from_shares(swap(scanned(spread_in, spread_in, width, False), "seq"), seqs * pairs)

    scan_out, sums = pl.pallas_call(
        partial(gate_kernel, per, head_size),
        grid=grid,
        in_specs=[wide, shared, pair, cols, wide, wide, lane_row],
        out_specs=[wide, two],
        out_shape=[like_float, shape(seqs, 2, block_len)],
        compiler_params=vmem(60),
    )(diag, read_map, incoming, col_pack, gate_pre, grad_normed, gain_row)
    sums = lax.psum(sums, "head")

    rows2 = pl.BlockSpec((1, 2, lanes), lambda s, g: (s, 0, g))
    normed_out, grad_scan, grad_gate_pre, state_term, gate_rows = pl.pallas_call(
        partial(back_kernel, per, head_size, inner_all),
        grid=grid,
        in_specs=[wide, wide, wide, lane_row, two, wide, shared, cols],
        out_specs=[wide, wide, wide, pair, rows2],
        out_shape=[like_values, like_values, like_values, like_states, shape(seqs, 2, inner)],
        compiler_params=vmem(60),
    )(scan_out, gate_pre, grad_normed, gain_row, sums, values, read_map, col_pack)

    spread_out = swap(to_shares(state_term, count), "seq")

    flat = lambda a: a.reshape(tokens, a.shape[-1])
    normed_flat, out_flat = flat(normed), flat(normed_out)
    grad_flat, ggate_flat = flat(grad_full), flat(grad_gate_pre)

    def product(left, right):
        half = left.shape[1] // 2

        def one(bit):
            return dot(columns(left, bit * half, half), right, 0, 0)

        return one

    summing = Summing("seq")
    early = product(out_flat, grad_flat), product(normed_flat, ggate_flat)
    early_sent, early_kept = summing.parts(*early)
    early_got = summing.traded(early_sent)

    grad_values, grad_read, grad_write, dcol, drow = pl.pallas_call(
        partial(mix_back_kernel, per, head_size),
        grid=grid,
        in_specs=[wide, wide, shared, shared, pair, cols, rows, lane_row],
        out_specs=[
            wide,
            shared,
            shared,
            pl.BlockSpec((1, 1, block_len, 2 * per), lambda s, g: (s, g, 0, 0)),
            pl.BlockSpec((1, 1, per, block_len), lambda s, g: (s, g, 0, 0)),
        ],
        out_shape=[
            like_float,
            like_map,
            like_map,
            shape(seqs, groups, block_len, 2 * per),
            shape(seqs, groups, per, block_len),
        ],
        scratch_shapes=[pltpu.VMEM((block_len, block_len), F32)],
        compiler_params=vmem(60),
    )(grad_scan, values, write_map, read_map, incoming, col_pack, row_pack, skip_row)

    spread_out, early_got, early_kept, _ = lax.optimization_barrier(
        (spread_out, early_got, early_kept, grad_values)
    )
    outgoing = swap(scanned(spread_out, spread_in, width, True), "seq")
    early_acc = summing.across(early_kept, early_got)
    outgoing, early_acc = lax.optimization_barrier((outgoing, early_acc))
    outgoing = from_shares(outgoing, seqs * pairs)
    rest = summing.rest
    if rest:
        early_acc = summing.halved(early_acc, rest[0])

    rows6 = pl.BlockSpec((1, 6, lanes), lambda s, g: (s, 0, g))
    grad_value_pre, tail_part, head_part, value_rows, grad_write, grad_end = pl.pallas_call(
        partial(state_back_kernel, per, head_size),
        grid=grid,
        in_specs=[
            pair, pair, wide, shared, cols, wide, shared, wide, prior, taps4, lane_row, valids,
        ],
        out_specs=[
            wide, prior, prior, rows6, shared,
            pl.BlockSpec((1, 1, block_len, per), lambda s, g: (s, g, 0, 0)),
        ],
        out_shape=[
            like_values,
            shape(seqs, PAD, inner),
            shape(seqs, PAD, inner),
            shape(seqs, 6, inner),
            like_map,
            shape(seqs, groups, block_len, per),
        ],
        compiler_params=vmem(60),
    )(
        outgoing, incoming, values, write_map, col_pack, grad_values, grad_write,
        value_pre, value_prior, conv_value, bias_row, valid,
    )

    early_acc, grad_value_pre, grad_write, tail_part, head_part, grad_end = lax.optimization_barrier(
        (early_acc, grad_value_pre, grad_write, tail_part, head_part, grad_end)
    )
    for mask in rest[1:]:
        early_acc = summing.halved(early_acc, mask)

    handed = jnp.where(core == 0, grad_read, grad_write)
    own_maps = jnp.where(core == 0, grad_write, grad_read)
    grad_maps = own_maps + lax.ppermute(handed, "head", [(0, 1), (1, 0)])
    maps_gext, grad_conv_maps, grad_maps_bias = maps_back(grad_maps)

    reach = kernel_len - 1
    halo = jnp.concatenate([head_part[:, PAD - reach :], maps_gext[:, :reach]], axis=-1)
    from_next = passed_along(halo, "seq", -1) * tail_keep
    tail_value = tail_part[:, PAD - reach :] + from_next[..., :inner]
    grad_value_pre = lax.dynamic_update_slice_in_dim(
        grad_value_pre, tail_value.astype(BF16), block_len - reach, 1
    )
    maps_gown = maps_gext[:, reach:]
    maps_gown = maps_gown.at[:, block_len - reach :].add(from_next[..., inner:])
    grad_maps_pre = maps_gown.astype(BF16)

    def all_of(*dims):
        return pl.BlockSpec((1, *dims), lambda s: (s,) + (0,) * len(dims))

    grad_step_pre, step_sums = pl.pallas_call(
        partial(unpack_kernel, groups),
        grid=(seqs,),
        in_specs=[
            each,
            whole_row,
            one_col,
            all_of(groups, block_len, 2 * per),
            all_of(groups, per, block_len),
            all_of(groups, block_len, per),
            all_of(6, inner),
        ],
        out_specs=[each, all_of(2, heads)],
        out_shape=[shape(seqs, block_len, heads, dtype=BF16), shape(seqs, 2, heads)],
        compiler_params=vmem(60),
    )(step_pre, log_row, seg_col, dcol, drow, grad_end, value_rows)
    grad_step_bias, grad_decay_log = jnp.sum(step_sums, axis=0)

    narrow = jnp.concatenate([grad_maps_pre, grad_step_pre], axis=-1)
    narrow = jnp.pad(narrow, ((0, 0), (0, 0), (0, -narrow.shape[-1] % LANES)))
    backward = list(reversed(rest))
    right = flat(jnp.concatenate([grad_value_pre, narrow], axis=-1))
    early_acc, right = lax.optimization_barrier((early_acc.astype(BF16), right))
    half = model_width // 2
    late = product(normed_flat[:, :half], right), product(normed_flat[:, half:], right)
    late_sent, late_kept = summing.parts(*late)
    late_got = summing.traded(late_sent)
    early_acc = after(early_acc, *late_sent)
    for mask in backward[:1]:
        early_acc = summing.grown(early_acc, mask)

    def pulled_back(rows_of):
        grads = (grad_gate_pre, proj_gate), (grad_value_pre, proj_value)
        grads += (grad_maps_pre, proj_maps), (grad_step_pre, proj_step)
        total = None
        for grad, weight in grads:
            part = jnp.einsum("sqk,dk->sqd", grad, rows_of(weight), preferred_element_type=F32)
            total = part if total is None else total + part
        return total

    def features(array, which, axis):
        return lax.dynamic_slice_in_dim(array, which * half_width, half_width, axis)

    weighing = gain_full * residual
    to_other = pulled_back(lambda w: features(w, 1 - core, 0))
    from_other = lax.ppermute(to_other, "head", [(0, 1), (1, 0)])
    mine = pulled_back(lambda w: features(w, core, 0))
    row_part = jnp.sum(to_other * features(weighing, 1 - core, 2), axis=-1, keepdims=True)
    row_part = row_part + jnp.sum(mine * features(weighing, core, 2), axis=-1, keepdims=True)
    row_sum = lax.psum(row_part, "head")
    grad_in_loc = mine + from_other

    late_got, late_kept, row_sum, early_acc = lax.optimization_barrier(
        (late_got, late_kept, row_sum, early_acc)
    )
    late_acc = summing.across(late_kept, late_got)
    for mask in backward[1:]:
        early_acc = summing.grown(early_acc, mask)
    hidden_loc = hidden_in.astype(F32)
    grad_norm_gain = jnp.sum(grad_in_loc * hidden_loc * inv_norm, axis=(0, 1))
    grad_normal = grad_in_loc * norm_gain.astype(F32)
    input_grad = (
        out_grad.astype(F32)
        + inv_norm * grad_normal
        - hidden_loc * (inv_norm * inv_norm * inv_norm) * (row_sum / model_width)
    )

    gate_rows = jnp.sum(gate_rows, axis=0)
    value_rows = jnp.sum(value_rows, axis=0)
    grad_gate_gain = gate_rows[0]
    grad_skip = jnp.sum(gate_rows[1].reshape(heads, head_size), axis=1)
    smalls = [
        grad_norm_gain,
        value_rows[:kernel_len],
        value_rows[kernel_len],
        grad_conv_maps,
        grad_maps_bias,
        grad_step_bias,
        grad_decay_log,
        grad_skip,
        grad_gate_gain,
    ]
    line = jnp.concatenate([a.reshape(-1) for a in smalls])
    across = right.shape[1]
    line = jnp.pad(line, (0, -line.shape[0] % (8 * across))).reshape(-1, across)

    late_acc, line, input_grad, early_acc = lax.optimization_barrier(
        (late_acc, line, input_grad, early_acc)
    )
    early_parts = summing.split(early_acc)
    normed_out = after(normed_out, late_acc)
    for mask in rest[:1]:
        late_acc, line = summing.halved(late_acc, mask, line)

    to_other = project(normed_out, features(proj_out, 1 - core, 1))
    from_other = lax.ppermute(to_other, "head", [(0, 1), (1, 0)])
    branch = project(normed_out, features(proj_out, core, 1)) + from_other
    mixed_out = (hidden_loc + branch).astype(BF16)

    late_acc, line, mixed_out, *early_parts = lax.optimization_barrier(
        (late_acc, line, mixed_out, *early_parts)
    )
    sum_out, sum_gate = summing.whole(*early_parts)
    for mask in rest[1:]:
        late_acc, line = summing.halved(late_acc, mask, line)

    late_acc = late_acc.astype(BF16)
    line = line + flip(line, "seq", 1)
    for mask in backward:
        late_acc = summing.grown(late_acc, mask)
    grad_proj_out, grad_proj_gate = sum_out.astype(F32), sum_gate.astype(F32)
    (sum_a, line), sum_b = summing.split(late_acc, line)
    line = line.reshape(-1)
    got_a, got_b = flip(sum_a, "seq", 1), flip(sum_b, "seq", 2)
    maps_end = inner + proj_maps.shape[1]

    def cut(start, stop):
        part = slice(start, stop)
        whole_a = ordered(sum_a[:, part], got_a[:, part], summing.bit(1))
        whole_b = ordered(sum_b[:, part], got_b[:, part], summing.bit(2))
        return jnp.concatenate([whole_a, whole_b], axis=0).astype(F32)

    grad_proj_value = cut(0, inner)
    grad_proj_maps = cut(inner, maps_end)
    grad_proj_step = cut(maps_end, maps_end + heads)

    found, start = [], 0
    for a in smalls:
        found.append(line[start : start + a.size].reshape(a.shape))
        start += a.size
    (
        grad_norm_gain,
        grad_conv_value,
        grad_value_bias,
        grad_conv_maps,
        grad_maps_bias,
        grad_step_bias,
        grad_decay_log,
        grad_skip,
        grad_gate_gain,
    ) = found
    return (
        mixed_out,
        input_grad,
        grad_norm_gain,
        grad_proj_gate,
        grad_proj_value,
        grad_proj_maps,
        grad_proj_step,
        grad_conv_value,
        grad_value_bias,
        grad_conv_maps,
        grad_maps_bias,
        grad_step_bias,
        grad_decay_log,
        grad_skip,
        grad_gate_gain,
        grad_proj_out,
    )


def solution(mesh):
    placed = (
        P(None, "seq", "head"),
        P(None, "seq"),
        P("head"),
        P(None, "head"),
        P(None, "head"),
        P(None, "head"),
        P(None, "head"),
        P(None, "head"),
        P("head"),
        P(None, "head"),
        P("head"),
        P("head"),
        P("head"),
        P("head"),
        P("head"),
        P("head", None),
        P(None, "seq", "head"),
    )
    return jax.shard_map(
        shards,
        mesh=mesh,
        in_specs=placed,
        out_specs=(
            P(None, "seq", "head"),
            P(None, "seq", "head"),
            P("head"),
            P(None, "head"),
            P(None, "head"),
            P(None, "head"),
            P(None, "head"),
            P(None, "head"),
            P("head"),
            P(None, "head"),
            P("head"),
            P("head"),
            P("head"),
            P("head"),
            P("head"),
            P("head", None),
        ),
        check_vma=False,
    )
```

```python
from functools import partial

import jax
import jax.numpy as jnp
from jax import lax
from jax.experimental import pallas as pl
from jax.experimental.pallas import tpu as pltpu
from jax.sharding import PartitionSpec as P

EPS = 1e-05
HIGHEST = lax.Precision.HIGHEST
F32 = jnp.float32
BF16 = jnp.bfloat16
LANES = 128
PAD = 16
NEVER = -1e30
EXTRA = 8


def passed_along(shard, axis, by):
    peers = lax.axis_size(axis)
    pairs = [(i, i + by) for i in range(peers) if 0 <= i + by < peers]
    return lax.ppermute(shard, axis, pairs)


def flip(shard, axis, mask):
    count = lax.axis_size(axis)
    return lax.ppermute(shard, axis, [(i, i ^ mask) for i in range(count)])


def dot(a, b, ca=1, cb=0):
    return lax.dot_general(a, b, (((ca,), (cb,)), ((), ())), preferred_element_type=F32)


def halves(a):
    high = a.astype(BF16)
    return high, (a - high.astype(F32)).astype(BF16)


def dot_wide(a, b, ca=1, cb=0):
    high, low = halves(a)
    return dot(high, b, ca, cb) + dot(low, b, ca, cb)


def dot_right(a, b, ca=1, cb=0):
    high, low = halves(b)
    return dot(jnp.concatenate([a, a], axis=ca), jnp.concatenate([high, low], axis=cb), ca, cb)


def dot_both(a, b, ca=1, cb=0):
    high, low = halves(b)
    return dot_wide(a, high, ca, cb) + dot(a.astype(BF16), low, ca, cb)


def silu_slope(source):
    sigmoid = jax.nn.sigmoid(source)
    return sigmoid * (1.0 + source * (1.0 - sigmoid))


def exact(a, b, ca=1, cb=0):
    return lax.dot_general(
        a, b, (((ca,), (cb,)), ((), ())), precision=HIGHEST, preferred_element_type=F32
    )


def triangle(size):
    later = lax.broadcasted_iota(jnp.int32, (size, size), 0)
    earlier = lax.broadcasted_iota(jnp.int32, (size, size), 1)
    return (later >= earlier).astype(F32), (later == earlier).astype(F32)


def spread_heads(heads, lanes):
    head = lax.broadcasted_iota(jnp.int32, (heads, lanes), 0)
    lane = lax.broadcasted_iota(jnp.int32, (heads, lanes), 1)
    return (lane // (lanes // heads) == head).astype(F32)


def decay_terms(pre, rate, seg, tril):
    step = jnp.maximum(pre, 0.0) + jnp.log1p(jnp.exp(-jnp.abs(pre)))
    cum = exact(tril, step * rate)
    last = cum[cum.shape[0] - 1 :]
    seg_last = seg[seg.shape[0] - 1 :]
    fresh = (seg == 0).astype(F32)
    end_plain = jnp.exp(last - cum) * (seg == seg_last).astype(F32)
    carry = jnp.exp(last) * (seg_last == 0).astype(F32)
    return step, cum, end_plain, jnp.exp(cum) * fresh, carry


def pack_kernel(groups, pairs, pre_ref, log_ref, seg_ref, col_ref, row_ref, decay_ref):
    pre, seg = pre_ref[0], seg_ref[0]
    block_len, heads = pre.shape
    per = heads // groups
    tril, eye = triangle(block_len)
    step, cum, end_plain, entry, carry = decay_terms(pre, -jnp.exp(log_ref[...]), seg, tril)
    end = end_plain * step
    segs = jnp.broadcast_to(seg, (block_len, per))
    turned = exact(jnp.concatenate([cum, step, segs], axis=1), eye, 0, 0)
    for g in range(groups):
        part = slice(g * per, (g + 1) * per)
        col_ref[0, g] = jnp.concatenate([cum[:, part], end[:, part], entry[:, part], segs], axis=1)
        row_ref[0, g] = jnp.concatenate(
            [turned[part], turned[heads + g * per : heads + (g + 1) * per], turned[2 * heads :]],
            axis=0,
        )
    lanes = exact(carry, spread_heads(heads, pairs * LANES))
    for j in range(pairs):
        decay_ref[j] = jnp.broadcast_to(lanes[:, j * LANES : (j + 1) * LANES], decay_ref.shape[1:])


def unpack_kernel(groups, pre_ref, log_ref, seg_ref, dcol_ref, drow_ref, gend_ref, rows_ref, out_ref, sums_ref):
    pre, seg = pre_ref[0], seg_ref[0]
    block_len, heads = pre.shape
    per = heads // groups
    tril, eye = triangle(block_len)
    rate = -jnp.exp(log_ref[...])
    step, cum, end_plain, entry, carry = decay_terms(pre, rate, seg, tril)
    dcum = jnp.concatenate([dcol_ref[0, g, :, :per] for g in range(groups)], axis=1)
    gentry = jnp.concatenate([dcol_ref[0, g, :, per:] for g in range(groups)], axis=1)
    gend = jnp.concatenate([gend_ref[0, g] for g in range(groups)], axis=1)
    from_row = exact(
        eye, jnp.concatenate([drow_ref[0, g] for g in range(groups)], axis=0), 1, 1
    )
    gcarry = rows_ref[0, rows_ref.shape[1] - 1 :]
    gcarry = exact(gcarry, spread_heads(heads, gcarry.shape[1]), 1, 1)
    ended = gend * (end_plain * step)
    at_last = jnp.sum(ended, axis=0, keepdims=True) + gcarry * carry
    grad_cum = dcum - from_row * step - ended + gentry * entry
    grad_rate = exact(tril, grad_cum, 0, 0) + at_last
    grad_step = (from_row + gend * end_plain + grad_rate * rate) * jax.nn.sigmoid(pre)
    out_ref[0] = grad_step.astype(BF16)
    by_log = jnp.sum(grad_rate * step, axis=0, keepdims=True) * rate
    sums_ref[0] = jnp.concatenate([jnp.sum(grad_step, axis=0, keepdims=True), by_log], axis=0)


def shifted(pre_ref, prior_ref):
    ext = jnp.concatenate([prior_ref[0].astype(F32), pre_ref[0].astype(F32)], axis=0)
    block_len = pre_ref.shape[1]
    return [ext[PAD - 3 + i : PAD - 3 + i + block_len] for i in range(4)]


def convolved(taps, kernel_ref, bias_ref, valid):
    summed = bias_ref[...]
    for i in range(4):
        summed = summed + kernel_ref[i : i + 1, :] * taps[i] * valid[:, i : i + 1]
    return summed


def column(col_ref, kind, a, per):
    return col_ref[0, 0, :, kind * per + a : kind * per + a + 1]


def by_head(col_ref, kind, per, head_size):
    lane = lax.broadcasted_iota(jnp.int32, (1, 2 * head_size), 1)
    parts = [
        jnp.where(lane < head_size, column(col_ref, kind, a, per), column(col_ref, kind, a + 1, per))
        for a in range(0, per, 2)
    ]
    return jnp.concatenate(parts, axis=1)


def head_parts(per, head_size):
    return [slice(a * head_size, (a + 1) * head_size) for a in range(per)]


def side(ref):
    return jnp.concatenate([ref[j] for j in range(ref.shape[0])], axis=1)


def local_kernel(per, head_size, pre_ref, prior_ref, kernel_ref, bias_ref, valid_ref, write_ref, col_ref, decay_ref, values_ref, state_ref):
    taps = shifted(pre_ref, prior_ref)
    summed = convolved(taps, kernel_ref, bias_ref, valid_ref[0])
    values = (summed * jax.nn.sigmoid(summed)).astype(BF16)
    values_ref[0] = values
    write = write_ref[0].astype(F32)
    width = write.shape[1]
    states = []
    for a, part in enumerate(head_parts(per, head_size)):
        weighted = (column(col_ref, 1, a, per) * write).astype(BF16)
        states.append(dot(weighted, values[:, part], 0, 0))
    for j in range(per // 2):
        state_ref[j, :width] = jnp.concatenate(states[2 * j : 2 * j + 2], axis=1)
        state_ref[j, width:] = decay_ref[j]


def kept_mask(seg_col, seg_row):
    block_len = seg_col.shape[0]
    later = lax.broadcasted_iota(jnp.int32, (block_len, block_len), 0)
    earlier = lax.broadcasted_iota(jnp.int32, (block_len, block_len), 1)
    return (later >= earlier) & (seg_col == seg_row)


def diag_kernel(per, head_size, values_ref, write_ref, read_ref, col_ref, row_ref, skip_ref, out_ref):
    scores = dot(read_ref[0], write_ref[0], 1, 1)
    keep = kept_mask(column(col_ref, 3, 0, per), row_ref[0, 0, 2 * per : 2 * per + 1, :])
    values = values_ref[0]
    outs = []
    for a, part in enumerate(head_parts(per, head_size)):
        spread = column(col_ref, 0, a, per) - row_ref[0, 0, a : a + 1, :]
        decay = jnp.exp(jnp.where(keep, spread, NEVER))
        mixing = (decay * scores * row_ref[0, 0, per + a : per + a + 1, :]).astype(BF16)
        outs.append(dot(mixing, values[:, part]))
    out_ref[0] = jnp.concatenate(outs, axis=1) + skip_ref[...] * values.astype(F32)


def gate_kernel(per, head_size, diag_ref, read_ref, inc_ref, col_ref, gate_ref, back_ref, gain_ref, scan_ref, sums_ref):
    carried = dot_right(read_ref[0], side(inc_ref))
    scan = diag_ref[0] + by_head(col_ref, 2, per, head_size) * carried
    scan_ref[0] = scan
    gate = gate_ref[0]
    prod = scan * (gate * jax.nn.sigmoid(gate))
    square = jnp.sum(prod * prod, axis=1, keepdims=True)
    inner = jnp.sum(back_ref[0] * gain_ref[...] * prod, axis=1, keepdims=True)
    both = jnp.concatenate([square, inner], axis=1)
    both = exact(both, triangle(both.shape[0])[1], 0, 0)

    @pl.when(pl.program_id(1) == 0)
    def _():
        sums_ref[0] = both

    @pl.when(pl.program_id(1) > 0)
    def _():
        sums_ref[0] += both


def back_kernel(per, head_size, inner_all, scan_ref, gate_ref, back_ref, gain_ref, sums_ref, values_ref, read_ref, col_ref, normed_ref, gscan_ref, ggate_ref, state_ref, rows_ref):
    sums = exact(triangle(sums_ref.shape[2])[1], sums_ref[0], 1, 1)
    inv = lax.rsqrt(sums[:, 0:1] / inner_all + EPS)
    inner = sums[:, 1:2] / inner_all
    scan, gate, back = scan_ref[0], gate_ref[0], back_ref[0]
    gain = gain_ref[...]
    sigmoid = jax.nn.sigmoid(gate)
    act = gate * sigmoid
    prod = scan * act
    gated_norm = prod * inv
    normed_ref[0] = (gated_norm * gain).astype(BF16)
    grad = inv * (back * gain) - prod * (inv * inv * inv * inner)
    gscan = (grad * act).astype(BF16)
    gscan_ref[0] = gscan
    ggate_ref[0] = (grad * scan * (sigmoid * (1.0 + gate * (1.0 - sigmoid)))).astype(BF16)
    gscan = gscan.astype(F32)
    gain_row = jnp.sum(back * gated_norm, axis=0, keepdims=True)
    skip_row = jnp.sum(gscan * values_ref[0].astype(F32), axis=0, keepdims=True)
    rows_ref[0] = jnp.concatenate([gain_row, skip_row], axis=0)
    entry = by_head(col_ref, 2, per, head_size) * gscan
    high, low = halves(entry)
    state = dot(read_ref[0], high, 0, 0) + dot(read_ref[0], low, 0, 0)
    for j in range(per // 2):
        state_ref[j] = state[:, j * LANES : (j + 1) * LANES]


def mix_back_kernel(per, head_size, gscan_ref, values_ref, write_ref, read_ref, inc_ref, col_ref, row_ref, skip_ref, gvalues_ref, gread_ref, gwrite_ref, dcol_ref, drow_ref, gscores_ref):
    turn = pl.program_id(1)
    scores = dot(read_ref[0], write_ref[0], 1, 1)
    keep = kept_mask(column(col_ref, 3, 0, per), row_ref[0, 0, 2 * per : 2 * per + 1, :])
    values, gscan = values_ref[0], gscan_ref[0]
    gscan_f = gscan.astype(F32)
    parts, cols, rows, total = [], [], [], None
    for a, part in enumerate(head_parts(per, head_size)):
        step = row_ref[0, 0, per + a : per + a + 1, :]
        spread = column(col_ref, 0, a, per) - row_ref[0, 0, a : a + 1, :]
        decay = jnp.exp(jnp.where(keep, spread, NEVER))
        mixing = (decay * scores * step).astype(BF16)
        parts.append(dot(mixing, gscan[:, part], 0, 0))
        pulled = dot(gscan[:, part], values[:, part], 1, 1) * decay
        stepped = pulled * step
        total = stepped if total is None else total + stepped
        cols.append(jnp.sum(stepped * scores, axis=1, keepdims=True))
        rows.append(jnp.sum(pulled * scores, axis=0, keepdims=True))
    gvalues_ref[0] = skip_ref[...] * gscan_f + jnp.concatenate(parts, axis=1)
    incoming = side(inc_ref)
    entered = gscan_f * dot_right(read_ref[0], incoming)
    entry = by_head(col_ref, 2, per, head_size) * gscan_f
    gread = dot_both(entry, incoming, 1, 1)
    for part in head_parts(per, head_size):
        cols.append(jnp.sum(entered[:, part], axis=1, keepdims=True))
    dcol_ref[0, 0] = jnp.concatenate(cols, axis=1)
    drow_ref[0, 0] = jnp.concatenate(rows, axis=0)

    @pl.when(turn == 0)
    def _():
        gread_ref[0] = gread
        gscores_ref[...] = total

    @pl.when(turn > 0)
    def _():
        gread_ref[0] += gread
        gscores_ref[...] += total

    @pl.when(turn == pl.num_programs(1) - 1)
    def _():
        gread_ref[0] += dot_wide(gscores_ref[...], write_ref[0])
        gwrite_ref[0] = dot_wide(gscores_ref[...], read_ref[0], 0, 0)


def state_back_kernel(per, head_size, out_ref, inc_ref, values_ref, write_ref, col_ref, gpart_ref, gwpart_ref, pre_ref, prior_ref, kernel_ref, bias_ref, valid_ref, gpre_ref, tail_ref, head_ref, rows_ref, gwrite_ref, gend_ref):
    turn = pl.program_id(1)
    outgoing = side(out_ref)
    out_high, out_low = halves(outgoing)
    values = values_ref[0]
    write = write_ref[0].astype(F32)
    parts, ends, total = [], [], None
    for a, part in enumerate(head_parts(per, head_size)):
        end = column(col_ref, 1, a, per)
        weighted = (end * write).astype(BF16)
        high, low = out_high[:, part], out_low[:, part]
        parts.append(dot(weighted, high) + dot(weighted, low))
        gweighted = dot(values[:, part], high, 1, 1) + dot(values[:, part], low, 1, 1)
        ends.append(jnp.sum(gweighted * write, axis=1, keepdims=True))
        total = gweighted * end if total is None else total + gweighted * end
    gend_ref[0, 0] = jnp.concatenate(ends, axis=1)

    @pl.when(turn == 0)
    def _():
        gwrite_ref[0] = gwpart_ref[0] + total

    @pl.when(turn > 0)
    def _():
        gwrite_ref[0] += total

    gvalues = gpart_ref[0] + jnp.concatenate(parts, axis=1)
    taps = shifted(pre_ref, prior_ref)
    valid = valid_ref[0]
    source = convolved(taps, kernel_ref, bias_ref, valid)
    grad = gvalues * silu_slope(source)
    block_len = grad.shape[0]
    blank = jnp.zeros((PAD, grad.shape[1]), F32)
    rows, summed = [], None
    for i in range(4):
        held = grad * valid[:, i : i + 1]
        rows.append(jnp.sum(held * taps[i], axis=0, keepdims=True))
        padded = jnp.concatenate([blank, kernel_ref[i : i + 1, :] * held, blank], axis=0)
        moved = padded[3 - i : 3 - i + block_len + PAD]
        summed = moved if summed is None else summed + moved
    rows.append(jnp.sum(grad, axis=0, keepdims=True))
    rows.append(jnp.sum(outgoing * side(inc_ref), axis=0, keepdims=True))
    rows_ref[0] = jnp.concatenate(rows, axis=0)
    head_ref[0] = summed[:PAD]
    own = summed[PAD:]
    gpre_ref[0] = own.astype(BF16)
    tail_ref[0] = own[block_len - PAD :]


def final_kernel(inner, maps_end, bits_ref, part_a, part_b, *refs):
    value_ref, maps_ref, step_ref = refs[-3:]
    for turn, source in enumerate((part_a, part_b)):

        @pl.when(pl.program_id(0) == turn)
        def _(source=source):
            value_ref[...] = source[:, :inner].astype(F32)
            maps_ref[...] = source[:, inner:maps_end].astype(F32)
            step_ref[...] = source[:, maps_end : maps_end + step_ref.shape[1]].astype(F32)


def scan_kernel(reverse, width, states_ref, decay_ref, out_ref):
    count = states_ref.shape[0]

    def one(turn, carried):
        block = count - 1 - turn if reverse else turn
        out_ref[pl.ds(block, 1)] = carried[None]
        decay = decay_ref[pl.ds(block, 1)][0, width : width + 1]
        return decay * carried + states_ref[pl.ds(block, 1)][0, :width]

    lax.fori_loop(0, count, one, jnp.zeros(out_ref.shape[1:], F32))


def vmem(mib):
    return pltpu.CompilerParams(vmem_limit_bytes=mib << 20)


def scanned(states, decays, width, reverse):
    count, _, share = states.shape
    return pl.pallas_call(
        partial(scan_kernel, reverse, width),
        out_shape=jax.ShapeDtypeStruct((count, width, share), F32),
        compiler_params=vmem(60),
    )(states, decays)


def to_shares(rows, count):
    pairs, width, lanes = rows.shape
    if pairs == count:
        return rows
    cut = count // pairs
    split = rows.reshape(pairs, width, cut, lanes // cut)
    return jnp.transpose(split, (0, 2, 1, 3)).reshape(count, width, lanes // cut)


def from_shares(shares, pairs):
    count, width, share = shares.shape
    if pairs == count:
        return shares
    cut = count // pairs
    split = shares.reshape(pairs, cut, width, share)
    return jnp.transpose(split, (0, 2, 1, 3)).reshape(pairs, width, cut * share)


def swap(shares, axis):
    return lax.all_to_all(shares, axis, 0, 0, tiled=True)


def ordered(own, got, bit):
    return jnp.where(
        bit == 0, jnp.concatenate([own, got], axis=0), jnp.concatenate([got, own], axis=0)
    )


class Summing:
    def __init__(self, axis):
        self.axis = axis
        count = lax.axis_size(axis)
        self.place = lax.axis_index(axis)
        self.rest = [1 << b for b in range(2, count.bit_length() - 1)]

    def bit(self, mask):
        return (self.place & mask) // mask

    def halved(self, acc, mask, rider=None):
        piece = acc.shape[0] // 2
        bit = self.bit(mask)
        sent = lax.dynamic_slice_in_dim(acc, (1 - bit) * piece, piece, 0)
        kept = lax.dynamic_slice_in_dim(acc, bit * piece, piece, 0)
        if rider is None:
            return kept + flip(sent, self.axis, mask)
        got = flip(jnp.concatenate([sent, rider], axis=0), self.axis, mask)
        return kept + got[:piece], rider + got[piece:]

    def parts(self, product_a, product_b):
        bit_a, bit_b = self.bit(1), self.bit(2)
        sent = product_a(1 - bit_a).astype(BF16), product_b(1 - bit_b).astype(BF16)
        return sent, (product_a(bit_a), product_b(bit_b))

    def traded(self, sent):
        return flip(sent[0], self.axis, 1), flip(sent[1], self.axis, 2)

    def across(self, kept, got):
        acc_a, acc_b = [own + other.astype(F32) for own, other in zip(kept, got)]
        return self.halved_low(acc_a, 2), self.halved_low(acc_b, 1)

    def chosen(self, pair, mask, rider=None):
        bit = self.bit(mask)
        sent, kept = jnp.where(bit == 0, pair[1], pair[0]), jnp.where(bit == 0, pair[0], pair[1])
        if rider is None:
            return kept + flip(sent, self.axis, mask)
        got = flip(jnp.concatenate([sent, rider], axis=0), self.axis, mask)
        return kept + got[: sent.shape[0]], rider + got[sent.shape[0] :]

    def unchosen(self, own, mask):
        got, bit = flip(own, self.axis, mask), self.bit(mask)
        return jnp.where(bit == 0, own, got), jnp.where(bit == 0, got, own)

    def halved_low(self, acc, mask):
        piece = acc.shape[0] // 2
        bit = self.bit(mask)
        sent = lax.dynamic_slice_in_dim(acc, (1 - bit) * piece, piece, 0)
        kept = lax.dynamic_slice_in_dim(acc, bit * piece, piece, 0)
        return kept + flip(sent.astype(BF16), self.axis, mask).astype(F32)

    def grown(self, own, mask, rider=None):
        if rider is None:
            return ordered(own, flip(own, self.axis, mask), self.bit(mask))
        parts, rest = [], rider
        for _ in range(3):
            high = lax.reduce_precision(rest, 8, 7)
            parts.append(high.astype(BF16))
            rest = rest - high
        size = own.shape[0]
        got = flip(jnp.concatenate([own, *parts], axis=0), self.axis, mask)
        extra = got[size:].astype(F32).reshape(3, *rider.shape)
        return ordered(own, got[:size], self.bit(mask)), rider + (extra[0] + extra[1] + extra[2])

    def begun(self, acc, mask):
        piece = acc.shape[0] // 2
        bit = self.bit(mask)
        sent = lax.dynamic_slice_in_dim(acc, (1 - bit) * piece, piece, 0)
        kept = lax.dynamic_slice_in_dim(acc, bit * piece, piece, 0)
        return kept, flip(sent, self.axis, mask)

    def split(self, pair, rider=None):
        return self.grown(pair[0], 2, rider), self.grown(pair[1], 1)

    def whole(self, part_a, part_b, rider=None):
        return self.grown(part_a, 1, rider), self.grown(part_b, 2)


def together(core, own):
    other = lax.ppermute(own, "head", [(0, 1), (1, 0)])
    return jnp.where(
        core == 0,
        jnp.concatenate([own, other], axis=-1),
        jnp.concatenate([other, own], axis=-1),
    )


def after(array, *others):
    return lax.optimization_barrier((array, *others))[0]


def columns(array, start, size):
    return lax.dynamic_slice_in_dim(array, start, size, 1)


def shards(
    hidden_in,
    doc_start,
    norm_gain,
    proj_gate,
    proj_value,
    proj_maps,
    proj_step,
    conv_value,
    value_bias,
    conv_maps,
    maps_bias,
    step_bias,
    decay_log,
    skip_gain,
    gate_gain,
    proj_out,
    out_grad,
):
    core = lax.axis_index("head")
    count = lax.axis_size("seq")
    seqs, block_len, half_width = hidden_in.shape
    inner = proj_value.shape[1]
    heads = proj_step.shape[1]
    head_size = inner // heads
    kernel_len = conv_value.shape[0]
    head_devices = lax.axis_size("head")
    inner_all = inner * head_devices
    model_width = half_width * head_devices
    width = proj_maps.shape[1] * head_devices // 2
    pairs = inner // LANES
    tokens = seqs * block_len

    hidden_full = together(core, hidden_in)
    gain_full = lax.all_gather(norm_gain, "head", axis=0, tiled=True).astype(F32)

    tril = jnp.tril(jnp.ones((block_len, block_len), F32))
    segment = jnp.round(jnp.einsum("tq,sq->st", tril, doc_start.astype(F32), precision=HIGHEST))
    tail_starts = doc_start[:, block_len - (kernel_len - 1) :]
    after_tail = jnp.cumsum(tail_starts[:, ::-1], axis=1)[:, ::-1] - tail_starts
    tail_keep = (after_tail == 0).astype(F32)[..., None]
    tail_rows = hidden_full[:, block_len - (kernel_len - 1) :] * tail_keep.astype(BF16)
    prior_hidden = passed_along(tail_rows, "seq", 1)
    prior_hidden = jnp.pad(prior_hidden, ((0, 0), (PAD - (kernel_len - 1), 0), (0, 0)))
    segment_ext = jnp.concatenate([jnp.zeros((seqs, kernel_len - 1), F32), segment], axis=1)
    valid = jnp.stack(
        [segment_ext[:, i : i + block_len] == segment for i in range(kernel_len)], axis=-1
    ).astype(F32)

    def normalize(rows):
        residual = rows.astype(F32)
        inv = lax.rsqrt(jnp.mean(residual * residual, axis=-1, keepdims=True) + EPS)
        return residual, inv, (residual * inv * gain_full).astype(BF16)

    residual, inv_norm, normed = normalize(hidden_full)
    normed_prior = normalize(prior_hidden)[2]

    def project(rows, weight):
        return jnp.dot(rows, weight, preferred_element_type=F32)

    maps_pre = project(normed, proj_maps).astype(BF16)
    maps_prior = project(normed_prior, proj_maps).astype(BF16)
    step_pre = project(normed, proj_step) + step_bias
    value_pre = project(normed, proj_value).astype(BF16)
    value_prior = project(normed_prior, proj_value).astype(BF16)

    def convolve(extended, kernel, bias):
        summed = bias
        for i in range(kernel_len):
            summed = summed + kernel[i] * extended[:, i : i + block_len] * valid[..., i : i + 1]
        return jax.nn.silu(summed)

    maps_ext = jnp.concatenate(
        [maps_prior[:, PAD - (kernel_len - 1) :], maps_pre], axis=1
    ).astype(F32)
    maps_act, maps_back = jax.vjp(convolve, maps_ext, conv_maps, maps_bias)
    maps_all = lax.all_gather(maps_act.astype(BF16), "head", axis=2, tiled=True)
    write_map, read_map = maps_all[..., :width], maps_all[..., width:]

    groups = 2 if pairs % 2 == 0 else 1
    cut = pairs // groups
    per = heads // groups
    seg_col = segment[..., None]
    log_row = decay_log[None]
    each = pl.BlockSpec((1, block_len, heads), lambda s: (s, 0, 0))
    whole_row = pl.BlockSpec((1, heads), lambda s: (0, 0))
    one_col = pl.BlockSpec((1, block_len, 1), lambda s: (s, 0, 0))
    col_pack, row_pack, decay_rows = pl.pallas_call(
        partial(pack_kernel, groups, pairs),
        grid=(seqs,),
        in_specs=[each, whole_row, one_col],
        out_specs=[
            pl.BlockSpec((1, groups, block_len, 4 * per), lambda s: (s, 0, 0, 0)),
            pl.BlockSpec((1, groups, 3 * per, block_len), lambda s: (s, 0, 0, 0)),
            pl.BlockSpec((pairs, EXTRA, LANES), lambda s: (s, 0, 0)),
        ],
        out_shape=[
            jax.ShapeDtypeStruct((seqs, groups, block_len, 4 * per), F32),
            jax.ShapeDtypeStruct((seqs, groups, 3 * per, block_len), F32),
            jax.ShapeDtypeStruct((seqs * pairs, EXTRA, LANES), F32),
        ],
        compiler_params=vmem(60),
    )(step_pre, log_row, seg_col)
    skip_row = jnp.repeat(skip_gain, head_size)[None]
    bias_row = value_bias[None]
    gain_row = gate_gain[None]

    grid = (seqs, groups)
    lanes = cut * LANES
    wide = pl.BlockSpec((1, block_len, lanes), lambda s, g: (s, 0, g))
    prior = pl.BlockSpec((1, PAD, lanes), lambda s, g: (s, 0, g))
    shared = pl.BlockSpec((1, block_len, width), lambda s, g: (s, 0, 0))
    taps4 = pl.BlockSpec((kernel_len, lanes), lambda s, g: (0, g))
    lane_row = pl.BlockSpec((1, lanes), lambda s, g: (0, g))
    valids = pl.BlockSpec((1, block_len, kernel_len), lambda s, g: (s, 0, 0))
    cols = pl.BlockSpec((1, 1, block_len, 4 * per), lambda s, g: (s, g, 0, 0))
    rows = pl.BlockSpec((1, 1, 3 * per, block_len), lambda s, g: (s, g, 0, 0))
    pair = pl.BlockSpec((cut, width, LANES), lambda s, g: (s * groups + g, 0, 0))
    pair_ext = pl.BlockSpec((cut, width + EXTRA, LANES), lambda s, g: (s * groups + g, 0, 0))
    pair_tail = pl.BlockSpec((cut, EXTRA, LANES), lambda s, g: (s * groups + g, 0, 0))
    two = pl.BlockSpec((1, 2, block_len), lambda s, g: (s, 0, 0))

    def shape(*dims, dtype=F32):
        return jax.ShapeDtypeStruct(dims, dtype)

    like_values = shape(seqs, block_len, inner, dtype=BF16)
    like_float = shape(seqs, block_len, inner)
    like_states = shape(seqs * pairs, width, LANES)
    like_map = shape(seqs, block_len, width)

    values, payload = pl.pallas_call(
        partial(local_kernel, per, head_size),
        grid=grid,
        in_specs=[wide, prior, taps4, lane_row, valids, shared, cols, pair_tail],
        out_specs=[wide, pair_ext],
        out_shape=[like_values, shape(seqs * pairs, width + EXTRA, LANES)],
        compiler_params=vmem(60),
    )(value_pre, value_prior, conv_value, bias_row, valid, write_map, col_pack, decay_rows)

    spread_in = swap(to_shares(payload, count), "seq")

    gate_pre = project(normed, proj_gate)
    grad_full = together(core, out_grad)
    grad_normed = jnp.einsum("sqd,id->sqi", grad_full, proj_out, preferred_element_type=F32)
    diag = pl.pallas_call(
        partial(diag_kernel, per, head_size),
        grid=grid,
        in_specs=[wide, shared, shared, cols, rows, lane_row],
        out_specs=wide,
        out_shape=like_float,
        compiler_params=vmem(60),
    )(values, write_map, read_map, col_pack, row_pack, skip_row)

    spread_in = after(spread_in, gate_pre, grad_normed, row_pack)
    incoming = from_shares(swap(scanned(spread_in, spread_in, width, False), "seq"), seqs * pairs)

    scan_out, sums = pl.pallas_call(
        partial(gate_kernel, per, head_size),
        grid=grid,
        in_specs=[wide, shared, pair, cols, wide, wide, lane_row],
        out_specs=[wide, two],
        out_shape=[like_float, shape(seqs, 2, block_len)],
        compiler_params=vmem(60),
    )(diag, read_map, incoming, col_pack, gate_pre, grad_normed, gain_row)
    sums = lax.psum(sums, "head")

    rows2 = pl.BlockSpec((1, 2, lanes), lambda s, g: (s, 0, g))
    normed_out, grad_scan, grad_gate_pre, state_term, gate_rows = pl.pallas_call(
        partial(back_kernel, per, head_size, inner_all),
        grid=grid,
        in_specs=[wide, wide, wide, lane_row, two, wide, shared, cols],
        out_specs=[wide, wide, wide, pair, rows2],
        out_shape=[like_values, like_values, like_values, like_states, shape(seqs, 2, inner)],
        compiler_params=vmem(60),
    )(scan_out, gate_pre, grad_normed, gain_row, sums, values, read_map, col_pack)

    spread_out = swap(to_shares(state_term, count), "seq")

    flat = lambda a: a.reshape(tokens, a.shape[-1])
    normed_flat, out_flat = flat(normed), flat(normed_out)
    grad_flat, ggate_flat = flat(grad_full), flat(grad_gate_pre)

    def product(left, right):
        half = left.shape[1] // 2

        def one(bit):
            return dot(columns(left, bit * half, half), right, 0, 0)

        return one

    summing = Summing("seq")
    early = product(out_flat, grad_flat), product(normed_flat, ggate_flat)
    early_sent, early_kept = summing.parts(*early)
    early_got = summing.traded(early_sent)

    grad_values, grad_read, grad_write, dcol, drow = pl.pallas_call(
        partial(mix_back_kernel, per, head_size),
        grid=grid,
        in_specs=[wide, wide, shared, shared, pair, cols, rows, lane_row],
        out_specs=[
            wide,
            shared,
            shared,
            pl.BlockSpec((1, 1, block_len, 2 * per), lambda s, g: (s, g, 0, 0)),
            pl.BlockSpec((1, 1, per, block_len), lambda s, g: (s, g, 0, 0)),
        ],
        out_shape=[
            like_float,
            like_map,
            like_map,
            shape(seqs, groups, block_len, 2 * per),
            shape(seqs, groups, per, block_len),
        ],
        scratch_shapes=[pltpu.VMEM((block_len, block_len), F32)],
        compiler_params=vmem(60),
    )(grad_scan, values, write_map, read_map, incoming, col_pack, row_pack, skip_row)

    spread_out, early_got, early_kept, _ = lax.optimization_barrier(
        (spread_out, early_got, early_kept, grad_values)
    )
    outgoing = swap(scanned(spread_out, spread_in, width, True), "seq")
    early_acc = summing.across(early_kept, early_got)
    outgoing, *early_acc = lax.optimization_barrier((outgoing, *early_acc))
    outgoing = from_shares(outgoing, seqs * pairs)
    rest = summing.rest
    early_acc = summing.chosen(early_acc, rest[0])

    rows6 = pl.BlockSpec((1, 6, lanes), lambda s, g: (s, 0, g))
    grad_value_pre, tail_part, head_part, value_rows, grad_write, grad_end = pl.pallas_call(
        partial(state_back_kernel, per, head_size),
        grid=grid,
        in_specs=[
            pair, pair, wide, shared, cols, wide, shared, wide, prior, taps4, lane_row, valids,
        ],
        out_specs=[
            wide, prior, prior, rows6, shared,
            pl.BlockSpec((1, 1, block_len, per), lambda s, g: (s, g, 0, 0)),
        ],
        out_shape=[
            like_values,
            shape(seqs, PAD, inner),
            shape(seqs, PAD, inner),
            shape(seqs, 6, inner),
            like_map,
            shape(seqs, groups, block_len, per),
        ],
        compiler_params=vmem(60),
    )(
        outgoing, incoming, values, write_map, col_pack, grad_values, grad_write,
        value_pre, value_prior, conv_value, bias_row, valid,
    )

    early_acc, grad_value_pre, grad_write, tail_part, head_part, grad_end = lax.optimization_barrier(
        (early_acc, grad_value_pre, grad_write, tail_part, head_part, grad_end)
    )

    handed = jnp.where(core == 0, grad_read, grad_write)
    own_maps = jnp.where(core == 0, grad_write, grad_read)
    grad_maps = own_maps + lax.ppermute(handed, "head", [(0, 1), (1, 0)])
    maps_gext, grad_conv_maps, grad_maps_bias = maps_back(grad_maps)

    reach = kernel_len - 1
    halo = jnp.concatenate([head_part[:, PAD - reach :], maps_gext[:, :reach]], axis=-1)
    from_next = passed_along(halo, "seq", -1) * tail_keep
    tail_value = tail_part[:, PAD - reach :] + from_next[..., :inner]
    grad_value_pre = lax.dynamic_update_slice_in_dim(
        grad_value_pre, tail_value.astype(BF16), block_len - reach, 1
    )
    maps_gown = maps_gext[:, reach:]
    maps_gown = maps_gown.at[:, block_len - reach :].add(from_next[..., inner:])
    grad_maps_pre = maps_gown.astype(BF16)

    def all_of(*dims):
        return pl.BlockSpec((1, *dims), lambda s: (s,) + (0,) * len(dims))

    grad_step_pre, step_sums = pl.pallas_call(
        partial(unpack_kernel, groups),
        grid=(seqs,),
        in_specs=[
            each,
            whole_row,
            one_col,
            all_of(groups, block_len, 2 * per),
            all_of(groups, per, block_len),
            all_of(groups, block_len, per),
            all_of(6, inner),
        ],
        out_specs=[each, all_of(2, heads)],
        out_shape=[shape(seqs, block_len, heads, dtype=BF16), shape(seqs, 2, heads)],
        compiler_params=vmem(60),
    )(step_pre, log_row, seg_col, dcol, drow, grad_end, value_rows)
    grad_step_bias, grad_decay_log = jnp.sum(step_sums, axis=0)

    narrow = jnp.concatenate([grad_maps_pre, grad_step_pre], axis=-1)
    narrow = jnp.pad(narrow, ((0, 0), (0, 0), (0, -narrow.shape[-1] % LANES)))
    backward = list(reversed(rest))
    right = flat(jnp.concatenate([grad_value_pre, narrow], axis=-1))
    half = model_width // 2
    late = product(normed_flat[:, :half], right), product(normed_flat[:, half:], right)
    late_sent, late_kept = summing.parts(*late)
    late_got = summing.traded(late_sent)
    early_acc = after(early_acc, *late_sent)
    for mask in rest[1:-1]:
        early_acc = summing.halved(early_acc, mask)
    early_kept, early_got = summing.begun(early_acc, rest[-1])

    def pulled_back(rows_of):
        grads = (grad_gate_pre, proj_gate), (grad_value_pre, proj_value)
        grads += (grad_maps_pre, proj_maps), (grad_step_pre, proj_step)
        total = None
        for grad, weight in grads:
            part = jnp.einsum("sqk,dk->sqd", grad, rows_of(weight), preferred_element_type=F32)
            total = part if total is None else total + part
        return total

    def features(array, which, axis):
        return lax.dynamic_slice_in_dim(array, which * half_width, half_width, axis)

    weighing = gain_full * residual
    to_other = pulled_back(lambda w: features(w, 1 - core, 0))
    from_other = lax.ppermute(to_other, "head", [(0, 1), (1, 0)])
    mine = pulled_back(lambda w: features(w, core, 0))
    row_part = jnp.sum(to_other * features(weighing, 1 - core, 2), axis=-1, keepdims=True)
    row_part = row_part + jnp.sum(mine * features(weighing, core, 2), axis=-1, keepdims=True)
    row_sum = lax.psum(row_part, "head")
    grad_in_loc = mine + from_other

    late_got, late_kept, row_sum = lax.optimization_barrier((late_got, late_kept, row_sum))
    late_acc = summing.across(late_kept, late_got)
    hidden_loc = hidden_in.astype(F32)
    grad_norm_gain = jnp.sum(grad_in_loc * hidden_loc * inv_norm, axis=(0, 1))
    grad_normal = grad_in_loc * norm_gain.astype(F32)
    input_grad = (
        out_grad.astype(F32)
        + inv_norm * grad_normal
        - hidden_loc * (inv_norm * inv_norm * inv_norm) * (row_sum / model_width)
    )

    gate_rows = jnp.sum(gate_rows, axis=0)
    value_rows = jnp.sum(value_rows, axis=0)
    grad_gate_gain = gate_rows[0]
    grad_skip = jnp.sum(gate_rows[1].reshape(heads, head_size), axis=1)
    smalls = [
        grad_norm_gain,
        value_rows[:kernel_len],
        value_rows[kernel_len],
        grad_conv_maps,
        grad_maps_bias,
        grad_step_bias,
        grad_decay_log,
        grad_skip,
        grad_gate_gain,
    ]
    line = jnp.concatenate([a.reshape(-1) for a in smalls])
    across = right.shape[1]
    line = jnp.pad(line, (0, -line.shape[0] % (8 * across))).reshape(-1, across)

    late_acc, line, input_grad, early_kept, early_got = lax.optimization_barrier(
        (late_acc, line, input_grad, early_kept, early_got)
    )
    normed_out = after(normed_out, *late_acc)
    late_acc, line = summing.chosen(late_acc, rest[0], line)
    early_acc = summing.grown((early_kept + early_got).astype(BF16), backward[0])

    to_other = project(normed_out, features(proj_out, 1 - core, 1))
    from_other = lax.ppermute(to_other, "head", [(0, 1), (1, 0)])
    branch = project(normed_out, features(proj_out, core, 1)) + from_other
    mixed_out = (hidden_loc + branch).astype(BF16)

    late_acc, line, mixed_out, early_acc = lax.optimization_barrier(
        (late_acc, line, mixed_out, early_acc)
    )
    for mask in rest[1:]:
        late_acc, line = summing.halved(late_acc, mask, line)
    for mask in backward[1:-1]:
        early_acc = summing.grown(early_acc, mask)
    early_pair = summing.unchosen(early_acc, rest[0])

    late_acc, early_pair = lax.optimization_barrier((late_acc.astype(BF16), early_pair))
    line = line + flip(line, "seq", 1)
    for mask in backward[:-1]:
        late_acc = summing.grown(late_acc, mask)
    early_parts = summing.split(early_pair)
    late_pair = summing.unchosen(late_acc, rest[0])
    sum_out, sum_gate = summing.whole(*early_parts)
    late_pair, sum_out, sum_gate = lax.optimization_barrier((late_pair, sum_out, sum_gate))
    grad_proj_out, grad_proj_gate = sum_out.astype(F32), sum_gate.astype(F32)
    (sum_a, line), sum_b = summing.split(late_pair, line)
    line = line.reshape(-1)
    got_a, got_b = flip(sum_a, "seq", 1), flip(sum_b, "seq", 2)
    maps_end = inner + proj_maps.shape[1]

    bits = jnp.stack([summing.bit(1), summing.bit(2)]).astype(jnp.int32)
    third = sum_a.shape[0]

    def finished(turn, part_a, part_b, *before):
        def row_block(i, bits_ref):
            bit = bits_ref[i]
            return (2 * i + bit + turn - 2 * bit * turn, 0)

        whole_part = pl.BlockSpec(sum_a.shape, lambda i, bits_ref: (0, 0))
        kept = [pl.BlockSpec(memory_space=pl.ANY)] * len(before)
        return pl.pallas_call(
            partial(final_kernel, inner, maps_end),
            grid_spec=pltpu.PrefetchScalarGridSpec(
                num_scalar_prefetch=1,
                grid=(2,),
                in_specs=[whole_part] * 2 + kept,
                out_specs=[
                    pl.BlockSpec((third, inner), row_block),
                    pl.BlockSpec((third, maps_end - inner), row_block),
                    pl.BlockSpec((third, heads), row_block),
                ],
            ),
            out_shape=[
                shape(model_width, inner),
                shape(model_width, maps_end - inner),
                shape(model_width, heads),
            ],
            input_output_aliases={3 + k: k for k in range(len(before))},
            compiler_params=vmem(60),
        )(bits, part_a, part_b, *before)

    grad_proj_value, grad_proj_maps, grad_proj_step = finished(
        1, got_a, got_b, *finished(0, sum_a, sum_b)
    )

    found, start = [], 0
    for a in smalls:
        found.append(line[start : start + a.size].reshape(a.shape))
        start += a.size
    (
        grad_norm_gain,
        grad_conv_value,
        grad_value_bias,
        grad_conv_maps,
        grad_maps_bias,
        grad_step_bias,
        grad_decay_log,
        grad_skip,
        grad_gate_gain,
    ) = found
    return (
        mixed_out,
        input_grad,
        grad_norm_gain,
        grad_proj_gate,
        grad_proj_value,
        grad_proj_maps,
        grad_proj_step,
        grad_conv_value,
        grad_value_bias,
        grad_conv_maps,
        grad_maps_bias,
        grad_step_bias,
        grad_decay_log,
        grad_skip,
        grad_gate_gain,
        grad_proj_out,
    )


def solution(mesh):
    placed = (
        P(None, "seq", "head"),
        P(None, "seq"),
        P("head"),
        P(None, "head"),
        P(None, "head"),
        P(None, "head"),
        P(None, "head"),
        P(None, "head"),
        P("head"),
        P(None, "head"),
        P("head"),
        P("head"),
        P("head"),
        P("head"),
        P("head"),
        P("head", None),
        P(None, "seq", "head"),
    )
    return jax.shard_map(
        shards,
        mesh=mesh,
        in_specs=placed,
        out_specs=(
            P(None, "seq", "head"),
            P(None, "seq", "head"),
            P("head"),
            P(None, "head"),
            P(None, "head"),
            P(None, "head"),
            P(None, "head"),
            P(None, "head"),
            P("head"),
            P(None, "head"),
            P("head"),
            P("head"),
            P("head"),
            P("head"),
            P("head"),
            P("head", None),
        ),
        check_vma=False,
    )
```
